32 devices in a mesh: chan: 8 (over y, x, core), seg: 4 (over z).
Axes of the slice: x: 2, y: 2, z: 4, core: 2. Of those that a mesh axis runs over, the one named last changes fastest.
Arguments:
- traces: bfloat16 [1024, 8, 8192], P('chan', 'seg'), may hold values from -20 to 20
- pair_offsets: int32 [8, 7], replicated, may hold values from 1 to 7, as said below
- pair_counts: int32 [8], replicated, may hold values from 1 to 7, 16 in all
- pair_owner: int32 [16], replicated, may hold values from 0 to 15, each once
Outputs:
- correlations: float32 [128, 16, 128, 256], P('seg', 'chan')
The draws below stay inside these ranges and needn't reach their ends.
Inputs may be any that keep to these rules, and one draw needn't show every extreme that they name: `pair_offsets`: row a lists 7 distinct offsets; only its first pair_counts[a] entries name pairs. `pair_counts`: the counts sum to 16. `pair_owner`: every slot number appears once.
All inputs are finite; a program needn't handle non-finite values.
Results may differ from the reference program's by a relative error of at most 0.017.
Values may be sent and summed in bfloat16 or wider, within the bound.
A program may use at most 128 MiB of HBM per device.

```python
import math
import jax
import jax.numpy as jnp
import numpy as np
from jax import lax

BLOCK = 128
SAMPLES = 8192
BAND_START = 32
FREQS = 512
HALF = 8
LAGS = 256
NBLK = 8
CHANNELS = 1024
SEGS = 8
SLOTS = 16
MAXOFF = 7


def draw_traces(key, part):
    gain_key, noise_key = jax.random.split(key, 2)
    gains = 10.0 ** jax.random.uniform(gain_key, (CHANNELS, 1, 1), jnp.float32, -2.5, 0.5)
    noise = jnp.clip(jax.random.normal(noise_key, (CHANNELS, SEGS, SAMPLES), jnp.float32), -6.0, 6.0)
    return (gains * noise).astype(jnp.bfloat16)


def draw_pair_offsets(key, part):
    row_keys = jax.random.split(key, NBLK)

    def one_row(row_key):
        return jax.random.permutation(row_key, NBLK - 1)[:MAXOFF] + 1
    return jax.vmap(one_row)(row_keys).astype(jnp.int32)


def split_up(number_of, total, most, slope):
    loads = [(1 << 20) // math.isqrt(grade ** slope) + 1 for grade in range(2, number_of + 1)]
    rest, holding = total - most - (number_of - 1), [1] * (number_of - 1)
    while rest > 0:
        movable = [i for i in range(number_of - 1) if holding[i] < most]
        pool, left = sum([loads[i] for i in movable]), rest
        for i in movable:
            addition = min(most - holding[i], max(1, left * loads[i] // pool), rest)
            holding[i] = holding[i] + addition
            rest = rest - addition
    return np.array([most] + holding)


def ragged(rng, count, total, bound, slope):
    if count == 2:
        one = jax.random.randint(rng, (), max(1, total - bound), min(bound, total - 1) + 1)
        return jnp.stack([one, total - one])
    sizes = jnp.asarray(split_up(count, total, bound, slope), jnp.int32)
    twos = (count - 1) // 2
    source_of, taker = sizes[1:1 + 2 * twos:2], sizes[2:2 + 2 * twos:2]
    room = jnp.minimum(source_of - 1, bound - taker)
    passed = jax.random.randint(jax.random.fold_in(rng, 1), (twos,), 0, 1 << 20) % (room + 1)
    sizes = sizes.at[1:1 + 2 * twos:2].set(source_of - passed).at[2:2 + 2 * twos:2].set(taker + passed)
    return sizes[jax.random.permutation(jax.random.fold_in(rng, 2), count)]


def setup_inputs(seed: int = 0) -> dict:
    streams_of = jax.random.split(jax.random.key(seed), 5)
    traces = draw_traces(jax.random.fold_in(streams_of[4], 71), 0)
    pair_offsets = draw_pair_offsets(jax.random.fold_in(streams_of[4], 71), 0)
    pair_counts = ragged(streams_of[2], NBLK, SLOTS, MAXOFF, 2).astype(jnp.int32)
    pair_owner = jax.random.permutation(streams_of[3], SLOTS).astype(jnp.int32)
    return {"traces": traces, "pair_offsets": pair_offsets, "pair_counts": pair_counts, "pair_owner": pair_owner}


def smoother(bin_count):
    bins_axis = lax.iota(jnp.int32, bin_count)
    nearby = (jnp.abs(bins_axis[:, None] - bins_axis[None, :]) <= HALF).astype(jnp.float32)
    return nearby / lax.optimization_barrier(jnp.sum(nearby, axis=0, keepdims=True))

def lag_table(first_bin, bin_count):
    bins_axis = BAND_START + first_bin + lax.iota(jnp.int32, bin_count)
    shifts = jnp.mod(lax.iota(jnp.int32, LAGS) - LAGS // 2, SAMPLES)
    phase_index = jnp.mod(bins_axis[:, None] * shifts[None, :], SAMPLES)
    angles = phase_index.astype(jnp.float32) * (2.0 * math.pi / SAMPLES)
    return jnp.concatenate([jnp.cos(angles), -jnp.sin(angles)], axis=0).astype(jnp.bfloat16)

def pair_blocks(pair_offsets, pair_counts, pair_owner, block_count, slot_count):
    slot_index = lax.iota(jnp.int32, slot_count)
    starts = (jnp.cumsum(pair_counts) - pair_counts).astype(jnp.int32)
    first_block = lax.optimization_barrier(jnp.sum((starts[None, :] <= slot_index[:, None]).astype(jnp.int32), axis=1)) - 1
    member = lax.iota(jnp.int32, block_count)[None, :] == first_block[:, None]
    start_of = lax.optimization_barrier(jnp.sum(jnp.where(member, starts[None, :], 0), axis=1))
    position = slot_index - start_of
    listed = lax.optimization_barrier(jnp.sum(jnp.where(member[:, :, None], pair_offsets[None, :, :], 0), axis=1))
    chosen = lax.iota(jnp.int32, pair_offsets.shape[1])[None, :] == position[:, None]
    offset = lax.optimization_barrier(jnp.sum(jnp.where(chosen, listed, 0), axis=1))
    second_block = jnp.mod(first_block + offset, block_count)
    held = pair_owner[None, :] == slot_index[:, None]
    slot_first = lax.optimization_barrier(jnp.sum(jnp.where(held, first_block[None, :], 0), axis=1)).astype(jnp.int32)
    slot_second = lax.optimization_barrier(jnp.sum(jnp.where(held, second_block[None, :], 0), axis=1)).astype(jnp.int32)
    return (slot_first, slot_second)

def whiten(block_traces):
    spectrum = jnp.fft.rfft(block_traces.astype(jnp.float32), axis=-1)[:, :, BAND_START:BAND_START + FREQS]
    real_part = jnp.real(spectrum)
    imag_part = jnp.imag(spectrum)
    amplitude = jnp.sqrt(real_part * real_part + imag_part * imag_part)
    smoothed = jnp.dot(amplitude.reshape(-1, FREQS), smoother(FREQS), precision=lax.Precision.HIGHEST).reshape(amplitude.shape)
    divisor = jnp.maximum(smoothed, 1.0)
    return jnp.stack([real_part / divisor, imag_part / divisor], axis=2).astype(jnp.bfloat16)

def reference(traces, pair_offsets, pair_counts, pair_owner):
    whitened = lax.map(whiten, traces.reshape(NBLK, BLOCK, SEGS, SAMPLES))
    slot_first, slot_second = pair_blocks(pair_offsets, pair_counts, pair_owner, NBLK, SLOTS)
    table = lag_table(0, FREQS)
    norm_factor = 1.0 / math.sqrt(FREQS * SEGS)

    def one_slot(blocks):
        first_spec = whitened[blocks[0]].astype(jnp.float32)
        second_spec = whitened[blocks[1]].astype(jnp.float32)
        turned = jnp.stack([first_spec[:, :, 1], -first_spec[:, :, 0]], axis=2)
        real_part = jnp.einsum('ispf,jspf->ijf', first_spec, second_spec, precision=lax.Precision.HIGHEST)
        imag_part = jnp.einsum('ispf,jspf->ijf', turned, second_spec, precision=lax.Precision.HIGHEST)
        cross = jnp.stack([real_part, imag_part], axis=2).astype(jnp.bfloat16)
        lagged = jnp.dot(cross.reshape(-1, 2 * FREQS), table, preferred_element_type=jnp.float32) * norm_factor
        return lagged.reshape(BLOCK, BLOCK, LAGS)
    stacked = lax.map(one_slot, jnp.stack([slot_first, slot_second], axis=1))
    return jnp.transpose(stacked, (1, 0, 2, 3))
```

```python
import functools
import math

import jax
import jax.numpy as jnp
import ml_dtypes
import numpy as np
from jax import lax
from jax.experimental import pallas as pl
from jax.experimental.pallas import tpu as pltpu
from jax.sharding import PartitionSpec as P

SAMPLES = 8192
BAND_START = 32
FREQS = 512
HALF = 8
LAGS = 256
TILE_DEV = 2

RADIX = 8
FOLDED = SAMPLES // RADIX
RESIDUES = (0, 4, 1, 7, 2, 6, 3, 5)
PER_RES = FREQS // RADIX
CHUNK = 256
STEPS = FOLDED // CHUNK
BF16 = ml_dtypes.bfloat16

BIN_ORDER = np.concatenate([np.arange(PER_RES) * RADIX + r for r in RESIDUES])


def dft_tables():
    n = np.arange(FOLDED)
    full = np.zeros((4, 4 * PER_RES, 2, FOLDED))
    for group in range(4):
        first, second = RESIDUES[2 * group], RESIDUES[2 * group + 1]
        parts = []
        for r in (first, second):
            k = BAND_START + np.arange(PER_RES) * RADIX + r
            angle = 2.0 * np.pi / SAMPLES * ((k[:, None] * n[None, :]) % SAMPLES)
            parts.append((np.cos(angle), np.sin(angle)))
        (c0, s0), (c1, s1) = parts
        o = np.zeros_like(c0)
        if group == 0:
            rows = [(c0, o), (-s0, o), (o, c1), (o, -s1)]
        else:
            rows = [(c0, s0), (-s0, c0), (c1, -s1), (-s1, -c1)]
        for i, (a, b) in enumerate(rows):
            full[group, i * PER_RES:(i + 1) * PER_RES, 0] = a
            full[group, i * PER_RES:(i + 1) * PER_RES, 1] = b
    full = full.reshape(4, 4 * PER_RES, 2, STEPS, CHUNK).transpose(3, 0, 1, 2, 4)
    full = full.reshape(STEPS, 4, 4 * PER_RES, 2 * CHUNK).astype(np.float32)
    high = full.astype(BF16)
    low = (full - high.astype(np.float32)).astype(BF16)
    return high, low


def lag_table():
    shifts = np.arange(LAGS) - LAGS // 2
    angle = 2.0 * np.pi / SAMPLES * (((BAND_START + BIN_ORDER)[None, :] * shifts[:, None]) % SAMPLES)
    return np.concatenate([np.cos(angle), -np.sin(angle)], axis=1).astype(np.float32).astype(BF16)


def window_tables():
    near = np.abs(BIN_ORDER[:, None] - BIN_ORDER[None, :]) <= HALF
    count = near.sum(axis=1).astype(np.float32)
    return near.astype(BF16), np.ascontiguousarray(np.broadcast_to(count[:, None], (FREQS, 256)))


def split(value):
    high = value.astype(jnp.bfloat16)
    return high, (value - high.astype(jnp.float32)).astype(jnp.bfloat16)


def dot_nt(a, b):
    return lax.dot_general(a, b, (((1,), (1,)), ((), ())), preferred_element_type=jnp.float32)


def dot_nn(a, b):
    return jnp.dot(a, b, preferred_element_type=jnp.float32)


def whiten_kernel(*refs):
    xs = refs[:RADIX]
    high_ref, low_ref, near_ref, count_ref, perm_ref, out_ref, total = refs[RADIX:]
    step = pl.program_id(0)

    @pl.when(step == 0)
    def _():
        total[...] = jnp.zeros_like(total)

    x = [ref[...].astype(jnp.float32) for ref in xs]
    e0, e1, e2, e3 = x[0] + x[4], x[1] + x[5], x[2] + x[6], x[3] + x[7]
    d0, d1, d2, d3 = x[0] - x[4], x[1] - x[5], x[2] - x[6], x[3] - x[7]
    root = math.sqrt(0.5)
    plus, minus = (d1 + d3) * root, (d1 - d3) * root
    folded = (
        ((e0 + e2) + (e1 + e3), (e0 + e2) - (e1 + e3)),
        (d0 + minus, -(d2 + plus)),
        (e0 - e2, e3 - e1),
        (d0 - minus, d2 - plus),
    )
    for group, (a, b) in enumerate(folded):
        a_high, a_low = split(a)
        b_high, b_low = split(b)
        y_high = jnp.concatenate([a_high, b_high], axis=1)
        y_low = jnp.concatenate([a_low, b_low], axis=1)
        t_high = high_ref[0, group]
        part = dot_nt(t_high, y_high) + dot_nt(t_high, y_low) + dot_nt(low_ref[0, group], y_high)
        total[group] += part

    @pl.when(step == STEPS - 1)
    def _():
        real, imag = [], []
        for group in range(4):
            for half in range(2):
                base = half * 2 * PER_RES
                real.append(total[group, base:base + PER_RES])
                imag.append(total[group, base + PER_RES:base + 2 * PER_RES])
        real = jnp.concatenate(real, axis=0)
        imag = jnp.concatenate(imag, axis=0)
        amplitude = jnp.sqrt(real * real + imag * imag)
        high, rest = amplitude.astype(jnp.bfloat16), None
        rest = amplitude - high.astype(jnp.float32)
        mid, low = split(rest)
        near = near_ref[...]
        summed = dot_nn(near, high) + (dot_nn(near, mid) + dot_nn(near, low))
        divisor = jnp.maximum(summed / count_ref[...], 1.0)
        segs = out_ref.shape[0]
        for part, value in enumerate((real, imag)):
            white = (value / divisor).astype(jnp.bfloat16)
            moved = dot_nn(white, perm_ref[...]).astype(jnp.bfloat16)
            width = moved.shape[1] // segs
            for s in range(segs):
                out_ref[s, part] = moved[:, s * width:(s + 1) * width]


def whiten(signal, block_size, segs):
    rows = block_size * segs
    high, low = dft_tables()
    near, count = window_tables()
    perm = np.zeros((rows, rows), np.float32)
    for c in range(block_size):
        for s in range(segs):
            perm[c * segs + s, s * block_size + c] = 1.0
    once = lambda shape: pl.BlockSpec(shape, lambda q: (0,) * len(shape))
    table = pl.BlockSpec((1, 4, 4 * PER_RES, 2 * CHUNK), lambda q: (q, 0, 0, 0))
    return pl.pallas_call(
        whiten_kernel,
        grid=(STEPS,),
        in_specs=[
            pl.BlockSpec((rows, CHUNK), functools.partial(lambda j, q: (0, j * STEPS + q), j))
            for j in range(RADIX)
        ] + [table, table, once((FREQS, FREQS)), once((FREQS, 256)), once((rows, rows))],
        out_specs=once((segs, 2, FREQS, block_size)),
        out_shape=jax.ShapeDtypeStruct((segs, 2, FREQS, block_size), jnp.bfloat16),
        scratch_shapes=[pltpu.VMEM((4, 4 * PER_RES, rows), jnp.float32)],
        compiler_params=pltpu.CompilerParams(vmem_limit_bytes=48 << 20),
    )(*([signal] * RADIX), jnp.asarray(high), jnp.asarray(low), jnp.asarray(near),
      jnp.asarray(count[:, :rows]), jnp.asarray(perm.astype(BF16)))


GROUP = 16
FCHUNK = 64
CROSS_STEPS = FREQS // FCHUNK
ROWS_STEP = 4


def stack_kernel(norm_factor, parts, segs, rows, index_ref, first_ref, second_ref, table_ref, out_ref, cross):
    step = pl.program_id(1)
    depth = parts * segs * 2 * GROUP
    block = second_ref.shape[-1]

    @pl.when(step < CROSS_STEPS)
    def _():
        own = index_ref[4] * rows
        select = (
            lax.broadcasted_iota(jnp.int32, (rows, block), 1)
            == lax.broadcasted_iota(jnp.int32, (rows, block), 0) + own
        ).astype(jnp.bfloat16)
        mask = (
            lax.broadcasted_iota(jnp.int32, (rows, GROUP, depth), 2) % GROUP
            == lax.broadcasted_iota(jnp.int32, (rows, GROUP, depth), 1)
        )
        for g in range(FCHUNK // GROUP):
            span = slice(g * GROUP, (g + 1) * GROUP)
            firsts, plain, turned = [], [], []
            for z in range(parts):
                for s in range(segs):
                    firsts += [first_ref[0, z, s, p, span] for p in range(2)]
                    re, im = second_ref[0, z, s, 0, span], second_ref[0, z, s, 1, span]
                    plain += [re, im]
                    turned += [-im, re]
            left = dot_nt(select, jnp.concatenate(firsts, axis=0))
            wide = jnp.broadcast_to(left[:, None, :], (rows, GROUP, depth))
            wide = jnp.where(mask, wide, 0.0).reshape(rows * GROUP, depth).astype(jnp.bfloat16)
            right = jnp.concatenate(
                [jnp.concatenate(plain, axis=0), jnp.concatenate(turned, axis=0)], axis=1
            )
            result = dot_nn(wide, right).astype(jnp.bfloat16).reshape(rows, GROUP, 2 * block)
            at = pl.multiple_of(step * FCHUNK + g * GROUP, GROUP)
            cross[:, 0, pl.ds(at, GROUP), :] = result[:, :, :block]
            cross[:, 1, pl.ds(at, GROUP), :] = result[:, :, block:]

    @pl.when(step >= CROSS_STEPS)
    def _():
        base = (step - CROSS_STEPS) * ROWS_STEP
        table = table_ref[...]
        for pair in range(ROWS_STEP // 2):
            both = [
                cross[base + 2 * pair + h].reshape(2 * FREQS, block) for h in range(2)
            ]
            lagged = dot_nn(table, jnp.concatenate(both, axis=1)) * norm_factor
            for h in range(2):
                out_ref[2 * pair + h, 0] = lagged[:, h * block:(h + 1) * block].T


def stack(index, gathered, norm_factor, rows):
    _, parts, segs, _, _, block = gathered.shape
    grid = (TILE_DEV, CROSS_STEPS + rows // ROWS_STEP)
    shape = (1, parts, segs, 2, FCHUNK, block)

    def place(offset, slot, step, index_ref):
        return (index_ref[offset + slot], 0, 0, 0, jnp.minimum(step, CROSS_STEPS - 1), 0)

    return pl.pallas_call(
        functools.partial(stack_kernel, norm_factor, parts, segs, rows),
        grid_spec=pltpu.PrefetchScalarGridSpec(
            num_scalar_prefetch=1,
            grid=grid,
            in_specs=[
                pl.BlockSpec(shape, functools.partial(place, 0)),
                pl.BlockSpec(shape, functools.partial(place, TILE_DEV)),
                pl.BlockSpec((LAGS, 2 * FREQS), lambda slot, step, index_ref: (0, 0)),
            ],
            out_specs=pl.BlockSpec(
                (ROWS_STEP, 1, block, LAGS),
                lambda slot, step, index_ref: (jnp.maximum(step - CROSS_STEPS, 0), slot, 0, 0),
            ),
            scratch_shapes=[pltpu.VMEM((rows, 2, FREQS, block), jnp.bfloat16)],
        ),
        out_shape=jax.ShapeDtypeStruct((rows, TILE_DEV, block, LAGS), jnp.float32),
        compiler_params=pltpu.CompilerParams(vmem_limit_bytes=48 << 20),
    )(index, gathered, gathered, jnp.asarray(lag_table()))


def pair_blocks(pair_offsets, pair_counts, pair_owner, block_count, slot_count):
    slot_index = lax.iota(jnp.int32, slot_count)
    starts = jnp.cumsum(pair_counts) - pair_counts
    first_block = jnp.sum((starts[None, :] <= slot_index[:, None]).astype(jnp.int32), axis=1) - 1
    member = lax.iota(jnp.int32, block_count)[None, :] == first_block[:, None]
    start_of = jnp.sum(jnp.where(member, starts[None, :], 0), axis=1)
    position = slot_index - start_of
    listed = jnp.sum(jnp.where(member[:, :, None], pair_offsets[None, :, :], 0), axis=1)
    chosen = lax.iota(jnp.int32, pair_offsets.shape[1])[None, :] == position[:, None]
    offset = jnp.sum(jnp.where(chosen, listed, 0), axis=1)
    second_block = jnp.mod(first_block + offset, block_count)
    held = pair_owner[None, :] == slot_index[:, None]
    slot_first = jnp.sum(jnp.where(held, first_block[None, :], 0), axis=1)
    slot_second = jnp.sum(jnp.where(held, second_block[None, :], 0), axis=1)
    return (slot_first, slot_second)


def on_device(traces, pair_offsets, pair_counts, pair_owner):
    block_size, local_segs, sample_count = traces.shape
    parts_count = lax.axis_size("seg")
    block_count = lax.axis_size("chan")
    norm_factor = 1.0 / math.sqrt(FREQS * local_segs * parts_count)
    signal = traces.reshape(block_size * local_segs, sample_count)
    whitened = whiten(signal, block_size, local_segs)
    gathered = lax.all_gather(lax.all_gather(whitened, "seg", axis=0), "chan", axis=0)
    slot_first, slot_second = pair_blocks(
        pair_offsets, pair_counts, pair_owner, block_count, pair_owner.shape[0]
    )
    my_start = lax.axis_index("chan") * TILE_DEV
    index = jnp.concatenate(
        [
            lax.dynamic_slice_in_dim(slot_first, my_start, TILE_DEV),
            lax.dynamic_slice_in_dim(slot_second, my_start, TILE_DEV),
            lax.axis_index("seg")[None],
        ]
    ).astype(jnp.int32)
    return stack(index, gathered, norm_factor, block_size // parts_count)


def solution(mesh):
    placed = (P("chan", "seg", None), P(), P(), P())
    return jax.shard_map(
        on_device,
        mesh=mesh,
        in_specs=placed,
        out_specs=P("seg", "chan", None, None),
        check_vma=False,
    )
```

```python
import functools
import math

import jax
import jax.numpy as jnp
import ml_dtypes
import numpy as np
from jax import lax
from jax.experimental import pallas as pl
from jax.experimental.pallas import tpu as pltpu
from jax.sharding import PartitionSpec as P

SAMPLES = 8192
BAND_START = 32
FREQS = 512
HALF = 8
LAGS = 256
TILE_DEV = 2

RADIX = 8
FOLDED = SAMPLES // RADIX
RESIDUES = (0, 4, 1, 7, 2, 6, 3, 5)
PER_RES = FREQS // RADIX
CHUNK = 256
STEPS = FOLDED // CHUNK
BF16 = ml_dtypes.bfloat16

BIN_ORDER = np.concatenate([np.arange(PER_RES) * RADIX + r for r in RESIDUES])


def dft_tables():
    n = np.arange(FOLDED)
    full = np.zeros((4, 4 * PER_RES, 2, FOLDED))
    for group in range(4):
        first, second = RESIDUES[2 * group], RESIDUES[2 * group + 1]
        parts = []
        for r in (first, second):
            k = BAND_START + np.arange(PER_RES) * RADIX + r
            angle = 2.0 * np.pi / SAMPLES * ((k[:, None] * n[None, :]) % SAMPLES)
            parts.append((np.cos(angle), np.sin(angle)))
        (c0, s0), (c1, s1) = parts
        o = np.zeros_like(c0)
        if group == 0:
            rows = [(c0, o), (-s0, o), (o, c1), (o, -s1)]
        else:
            rows = [(c0, s0), (-s0, c0), (c1, -s1), (-s1, -c1)]
        for i, (a, b) in enumerate(rows):
            full[group, i * PER_RES:(i + 1) * PER_RES, 0] = a
            full[group, i * PER_RES:(i + 1) * PER_RES, 1] = b
    full = full.reshape(4, 4 * PER_RES, 2, STEPS, CHUNK).transpose(3, 0, 1, 2, 4)
    full = full.reshape(STEPS, 4, 4 * PER_RES, 2 * CHUNK).astype(np.float32)
    high = full.astype(BF16)
    low = (full - high.astype(np.float32)).astype(BF16)
    return high, low


def lag_table():
    shifts = np.arange(LAGS) - LAGS // 2
    angle = 2.0 * np.pi / SAMPLES * (((BAND_START + BIN_ORDER)[None, :] * shifts[:, None]) % SAMPLES)
    return np.concatenate([np.cos(angle), -np.sin(angle)], axis=1).astype(np.float32).astype(BF16)


def window_tables():
    near = np.abs(BIN_ORDER[:, None] - BIN_ORDER[None, :]) <= HALF
    count = near.sum(axis=1).astype(np.float32)
    return near.astype(BF16), np.ascontiguousarray(np.broadcast_to(count[:, None], (FREQS, 256)))


def split(value):
    high = value.astype(jnp.bfloat16)
    return high, (value - high.astype(jnp.float32)).astype(jnp.bfloat16)


def dot_nt(a, b):
    return lax.dot_general(a, b, (((1,), (1,)), ((), ())), preferred_element_type=jnp.float32)


def dot_nn(a, b):
    return jnp.dot(a, b, preferred_element_type=jnp.float32)


def whiten_kernel(*refs):
    xs = refs[:RADIX]
    high_ref, low_ref, near_ref, count_ref, perm_ref, out_ref, total = refs[RADIX:]
    step = pl.program_id(0)

    @pl.when(step == 0)
    def _():
        total[...] = jnp.zeros_like(total)

    x = [ref[...].astype(jnp.float32) for ref in xs]
    e0, e1, e2, e3 = x[0] + x[4], x[1] + x[5], x[2] + x[6], x[3] + x[7]
    d0, d1, d2, d3 = x[0] - x[4], x[1] - x[5], x[2] - x[6], x[3] - x[7]
    root = math.sqrt(0.5)
    plus, minus = (d1 + d3) * root, (d1 - d3) * root
    folded = (
        ((e0 + e2) + (e1 + e3), (e0 + e2) - (e1 + e3)),
        (d0 + minus, -(d2 + plus)),
        (e0 - e2, e3 - e1),
        (d0 - minus, d2 - plus),
    )
    for group, (a, b) in enumerate(folded):
        a_high, a_low = split(a)
        b_high, b_low = split(b)
        y_high = jnp.concatenate([a_high, b_high], axis=1)
        y_low = jnp.concatenate([a_low, b_low], axis=1)
        t_high = high_ref[0, group]
        part = dot_nt(t_high, y_high) + dot_nt(t_high, y_low) + dot_nt(low_ref[0, group], y_high)
        total[group] += part

    @pl.when(step == STEPS - 1)
    def _():
        real, imag = [], []
        for group in range(4):
            for half in range(2):
                base = half * 2 * PER_RES
                real.append(total[group, base:base + PER_RES])
                imag.append(total[group, base + PER_RES:base + 2 * PER_RES])
        real = jnp.concatenate(real, axis=0)
        imag = jnp.concatenate(imag, axis=0)
        amplitude = jnp.sqrt(real * real + imag * imag)
        high, rest = amplitude.astype(jnp.bfloat16), None
        rest = amplitude - high.astype(jnp.float32)
        mid, low = split(rest)
        near = near_ref[...]
        summed = dot_nn(near, high) + (dot_nn(near, mid) + dot_nn(near, low))
        divisor = jnp.maximum(summed / count_ref[...], 1.0)
        segs = out_ref.shape[0]
        for part, value in enumerate((real, imag)):
            white = (value / divisor).astype(jnp.bfloat16)
            moved = dot_nn(white, perm_ref[...]).astype(jnp.bfloat16)
            width = moved.shape[1] // segs
            for s in range(segs):
                out_ref[s, part] = moved[:, s * width:(s + 1) * width]


def whiten(signal, block_size, segs):
    rows = block_size * segs
    high, low = dft_tables()
    near, count = window_tables()
    perm = np.zeros((rows, rows), np.float32)
    for c in range(block_size):
        for s in range(segs):
            perm[c * segs + s, s * block_size + c] = 1.0
    once = lambda shape: pl.BlockSpec(shape, lambda q: (0,) * len(shape))
    table = pl.BlockSpec((1, 4, 4 * PER_RES, 2 * CHUNK), lambda q: (q, 0, 0, 0))
    return pl.pallas_call(
        whiten_kernel,
        grid=(STEPS,),
        in_specs=[
            pl.BlockSpec((rows, CHUNK), functools.partial(lambda j, q: (0, j * STEPS + q), j))
            for j in range(RADIX)
        ] + [table, table, once((FREQS, FREQS)), once((FREQS, 256)), once((rows, rows))],
        out_specs=once((segs, 2, FREQS, block_size)),
        out_shape=jax.ShapeDtypeStruct((segs, 2, FREQS, block_size), jnp.bfloat16),
        scratch_shapes=[pltpu.VMEM((4, 4 * PER_RES, rows), jnp.float32)],
        compiler_params=pltpu.CompilerParams(vmem_limit_bytes=48 << 20),
    )(*([signal] * RADIX), jnp.asarray(high), jnp.asarray(low), jnp.asarray(near),
      jnp.asarray(count[:, :rows]), jnp.asarray(perm.astype(BF16)))


PLANES = 4
MESH = pl.DeviceIdType.MESH


def gather_kernel(own_ref, all_ref, z_send, z_recv, p_send, p_recv, c_send, c_recv, own_sem):
    chan, seg = lax.axis_index("chan"), lax.axis_index("seg")
    y, x, core = chan // 4, (chan // 2) % 2, chan % 2
    x_near = 4 * y + 2 * (1 - x) + core
    y_near = 4 * (1 - y) + 2 * x + core
    across = 4 * (1 - y) + 2 * (1 - x) + core
    twin = 4 * y + 2 * x + (1 - core)

    barrier = pltpu.get_barrier_semaphore()
    for other in (x_near, y_near, twin):
        pl.semaphore_signal(barrier, inc=1, device_id=(other, seg), device_id_type=MESH)

    def send(src, dst, send_sem, recv_sem, device):
        copy = pltpu.make_async_remote_copy(
            src_ref=src, dst_ref=dst, send_sem=send_sem, recv_sem=recv_sem,
            device_id=device, device_id_type=MESH,
        )
        copy.start()
        return copy

    def program(z):
        for step in (1, -1):
            if 0 <= z + step < PLANES:
                pl.semaphore_signal(barrier, inc=1, device_id=(chan, z + step), device_id_type=MESH)
        pl.semaphore_wait(barrier, 3 + (z > 0) + (z < PLANES - 1))
        sent = []
        order = sorted(range(PLANES), key=lambda other: abs(other - z))
        local = pltpu.make_async_copy(own_ref, all_ref.at[chan, z], own_sem)
        local.start()

        def piece(other):
            return own_ref if other == z else all_ref.at[chan, other]

        def along(other):
            for step, side in ((1, 0), (-1, 1)):
                away = other == z or (z - other) * step > 0
                if away and 0 <= z + step < PLANES:
                    sent.append(send(piece(other), all_ref.at[chan, other], z_send.at[other, side],
                                     z_recv.at[other], (chan, z + step)))

        def landed(ref, sem):
            pltpu.make_async_remote_copy(
                src_ref=ref, dst_ref=ref, send_sem=sem, recv_sem=sem,
                device_id=(twin, z), device_id_type=MESH,
            ).wait_recv()

        def to_twin(src, block, other, half, slot):
            sent.append(send(src, all_ref.at[block, other, half], c_send.at[other, slot, half],
                             c_recv.at[other, slot, half], (twin, z)))

        def outward(other):
            for half in (0, 1):
                for way, near in ((0, x_near), (1, y_near)):
                    part = half if way == 0 else 1 - half
                    sent.append(send(piece(other).at[part], all_ref.at[chan, other, part],
                                     p_send.at[other, way, part], p_recv.at[other, way, part], (near, z)))
            for half in (0, 1):
                to_twin(piece(other).at[half], chan, other, half, 0)

        def onward(other):
            for first in (0, 1):
                for way, block in ((0, x_near), (1, y_near)):
                    half = first if way == 0 else 1 - first
                    ref = all_ref.at[block, other, half]
                    landed(ref, p_recv.at[other, way, half])
                    if half == way:
                        sent.append(send(ref, ref, p_send.at[other, 2, half], p_recv.at[other, 2, half],
                                         ((y_near, x_near)[way], z)))
                    to_twin(ref, block, other, half, 1 + way)

        def finish(other):
            for half in (0, 1):
                ref = all_ref.at[across, other, half]
                landed(ref, p_recv.at[other, 2, half])
                to_twin(ref, across, other, half, 3)

        along(z)
        outward(z)
        for k in range(1, PLANES):
            landed(all_ref.at[chan, order[k]], z_recv.at[order[k]])
            along(order[k])
            outward(order[k])
            onward(order[k - 1])
            if k > 1:
                finish(order[k - 2])
        onward(order[-1])
        finish(order[-2])
        finish(order[-1])
        twin_blocks = [4 * y + 2 * x, 4 * y + 2 * (1 - x), 4 * (1 - y) + 2 * x, 4 * (1 - y) + 2 * (1 - x)]
        for other in range(PLANES):
            for slot, block in enumerate(twin_blocks):
                for half in (0, 1):
                    landed(all_ref.at[block + 1 - core, other, half], c_recv.at[other, slot, half])
        for copy in sent:
            copy.wait_send()
        local.wait()

    for z in range(PLANES):
        pl.when(seg == z)(functools.partial(program, z))


def gather(own):
    dma = pltpu.SemaphoreType.DMA
    return pl.pallas_call(
        gather_kernel,
        in_specs=[pl.BlockSpec(memory_space=pl.ANY)],
        out_specs=pl.BlockSpec(memory_space=pl.ANY),
        out_shape=jax.ShapeDtypeStruct((8, PLANES) + own.shape, own.dtype),
        scratch_shapes=[
            dma((PLANES, 2)), dma((PLANES,)),
            dma((PLANES, 3, 2)), dma((PLANES, 3, 2)),
            dma((PLANES, 4, 2)), dma((PLANES, 4, 2)), dma,
        ],
        compiler_params=pltpu.CompilerParams(collective_id=0, has_side_effects=True),
    )(own)


GROUP = 16
FCHUNK = 64
CROSS_STEPS = FREQS // FCHUNK
ROWS_STEP = 4


def stack_kernel(norm_factor, parts, segs, rows, index_ref, first_ref, second_ref, table_ref, out_ref, cross):
    step = pl.program_id(1)
    depth = parts * segs * 2 * GROUP
    block = second_ref.shape[-1]

    @pl.when(step < CROSS_STEPS)
    def _():
        own = index_ref[4] * rows
        select = (
            lax.broadcasted_iota(jnp.int32, (rows, block), 1)
            == lax.broadcasted_iota(jnp.int32, (rows, block), 0) + own
        ).astype(jnp.bfloat16)
        mask = (
            lax.broadcasted_iota(jnp.int32, (rows, GROUP, depth), 2) % GROUP
            == lax.broadcasted_iota(jnp.int32, (rows, GROUP, depth), 1)
        )
        for g in range(FCHUNK // GROUP):
            span = slice(g * GROUP, (g + 1) * GROUP)
            firsts, plain, turned = [], [], []
            for z in range(parts):
                for s in range(segs):
                    firsts += [first_ref[0, z, s, p, span] for p in range(2)]
                    re, im = second_ref[0, z, s, 0, span], second_ref[0, z, s, 1, span]
                    plain += [re, im]
                    turned += [-im, re]
            left = dot_nt(select, jnp.concatenate(firsts, axis=0))
            wide = jnp.broadcast_to(left[:, None, :], (rows, GROUP, depth))
            wide = jnp.where(mask, wide, 0.0).reshape(rows * GROUP, depth).astype(jnp.bfloat16)
            right = jnp.concatenate(
                [jnp.concatenate(plain, axis=0), jnp.concatenate(turned, axis=0)], axis=1
            )
            result = dot_nn(wide, right).astype(jnp.bfloat16).reshape(rows, GROUP, 2 * block)
            at = pl.multiple_of(step * FCHUNK + g * GROUP, GROUP)
            cross[:, 0, pl.ds(at, GROUP), :] = result[:, :, :block]
            cross[:, 1, pl.ds(at, GROUP), :] = result[:, :, block:]

    @pl.when(step >= CROSS_STEPS)
    def _():
        base = (step - CROSS_STEPS) * ROWS_STEP
        table = table_ref[...]
        for pair in range(ROWS_STEP // 2):
            both = [
                cross[base + 2 * pair + h].reshape(2 * FREQS, block) for h in range(2)
            ]
            lagged = dot_nn(table, jnp.concatenate(both, axis=1)) * norm_factor
            for h in range(2):
                out_ref[2 * pair + h, 0] = lagged[:, h * block:(h + 1) * block].T


def stack(index, gathered, norm_factor, rows):
    _, parts, segs, _, _, block = gathered.shape
    grid = (TILE_DEV, CROSS_STEPS + rows // ROWS_STEP)
    shape = (1, parts, segs, 2, FCHUNK, block)

    def place(offset, slot, step, index_ref):
        return (index_ref[offset + slot], 0, 0, 0, jnp.minimum(step, CROSS_STEPS - 1), 0)

    return pl.pallas_call(
        functools.partial(stack_kernel, norm_factor, parts, segs, rows),
        grid_spec=pltpu.PrefetchScalarGridSpec(
            num_scalar_prefetch=1,
            grid=grid,
            in_specs=[
                pl.BlockSpec(shape, functools.partial(place, 0)),
                pl.BlockSpec(shape, functools.partial(place, TILE_DEV)),
                pl.BlockSpec((LAGS, 2 * FREQS), lambda slot, step, index_ref: (0, 0)),
            ],
            out_specs=pl.BlockSpec(
                (ROWS_STEP, 1, block, LAGS),
                lambda slot, step, index_ref: (jnp.maximum(step - CROSS_STEPS, 0), slot, 0, 0),
            ),
            scratch_shapes=[pltpu.VMEM((rows, 2, FREQS, block), jnp.bfloat16)],
        ),
        out_shape=jax.ShapeDtypeStruct((rows, TILE_DEV, block, LAGS), jnp.float32),
        compiler_params=pltpu.CompilerParams(vmem_limit_bytes=48 << 20),
    )(index, gathered, gathered, jnp.asarray(lag_table()))


def pair_blocks(pair_offsets, pair_counts, pair_owner, block_count, slot_count):
    slot_index = lax.iota(jnp.int32, slot_count)
    starts = jnp.cumsum(pair_counts) - pair_counts
    first_block = jnp.sum((starts[None, :] <= slot_index[:, None]).astype(jnp.int32), axis=1) - 1
    member = lax.iota(jnp.int32, block_count)[None, :] == first_block[:, None]
    start_of = jnp.sum(jnp.where(member, starts[None, :], 0), axis=1)
    position = slot_index - start_of
    listed = jnp.sum(jnp.where(member[:, :, None], pair_offsets[None, :, :], 0), axis=1)
    chosen = lax.iota(jnp.int32, pair_offsets.shape[1])[None, :] == position[:, None]
    offset = jnp.sum(jnp.where(chosen, listed, 0), axis=1)
    second_block = jnp.mod(first_block + offset, block_count)
    held = pair_owner[None, :] == slot_index[:, None]
    slot_first = jnp.sum(jnp.where(held, first_block[None, :], 0), axis=1)
    slot_second = jnp.sum(jnp.where(held, second_block[None, :], 0), axis=1)
    return (slot_first, slot_second)


def on_device(traces, pair_offsets, pair_counts, pair_owner):
    block_size, local_segs, sample_count = traces.shape
    parts_count = lax.axis_size("seg")
    block_count = lax.axis_size("chan")
    norm_factor = 1.0 / math.sqrt(FREQS * local_segs * parts_count)
    signal = traces.reshape(block_size * local_segs, sample_count)
    whitened = whiten(signal, block_size, local_segs)
    if (block_count, parts_count) == (8, PLANES):
        gathered = gather(whitened)
    else:
        gathered = lax.all_gather(lax.all_gather(whitened, "seg", axis=0), "chan", axis=0)
    slot_first, slot_second = pair_blocks(
        pair_offsets, pair_counts, pair_owner, block_count, pair_owner.shape[0]
    )
    my_start = lax.axis_index("chan") * TILE_DEV
    index = jnp.concatenate(
        [
            lax.dynamic_slice_in_dim(slot_first, my_start, TILE_DEV),
            lax.dynamic_slice_in_dim(slot_second, my_start, TILE_DEV),
            lax.axis_index("seg")[None],
        ]
    ).astype(jnp.int32)
    return stack(index, gathered, norm_factor, block_size // parts_count)


def solution(mesh):
    placed = (P("chan", "seg", None), P(), P(), P())
    return jax.shard_map(
        on_device,
        mesh=mesh,
        in_specs=placed,
        out_specs=P("seg", "chan", None, None),
        check_vma=False,
    )
```

```python
import functools
import math

import jax
import jax.numpy as jnp
import ml_dtypes
import numpy as np
from jax import lax
from jax.experimental import pallas as pl
from jax.experimental.pallas import tpu as pltpu
from jax.sharding import PartitionSpec as P

SAMPLES = 8192
BAND_START = 32
FREQS = 512
HALF = 8
LAGS = 256
TILE_DEV = 2

RADIX = 8
FOLDED = SAMPLES // RADIX
RESIDUES = (0, 4, 1, 7, 2, 6, 3, 5)
PER_RES = FREQS // RADIX
CHUNK = 256
STEPS = FOLDED // CHUNK
BF16 = ml_dtypes.bfloat16

BIN_ORDER = np.concatenate([np.arange(PER_RES) * RADIX + r for r in RESIDUES])


def dft_tables():
    n = np.arange(FOLDED)
    full = np.zeros((4, 4 * PER_RES, 2, FOLDED))
    for group in range(4):
        first, second = RESIDUES[2 * group], RESIDUES[2 * group + 1]
        parts = []
        for r in (first, second):
            k = BAND_START + np.arange(PER_RES) * RADIX + r
            angle = 2.0 * np.pi / SAMPLES * ((k[:, None] * n[None, :]) % SAMPLES)
            parts.append((np.cos(angle), np.sin(angle)))
        (c0, s0), (c1, s1) = parts
        o = np.zeros_like(c0)
        if group == 0:
            rows = [(c0, o), (-s0, o), (o, c1), (o, -s1)]
        else:
            rows = [(c0, s0), (-s0, c0), (c1, -s1), (-s1, -c1)]
        for i, (a, b) in enumerate(rows):
            full[group, i * PER_RES:(i + 1) * PER_RES, 0] = a
            full[group, i * PER_RES:(i + 1) * PER_RES, 1] = b
    full = full.reshape(4, 4 * PER_RES, 2, STEPS, CHUNK).transpose(3, 0, 1, 2, 4)
    full = full.reshape(STEPS, 4, 4 * PER_RES, 2 * CHUNK).astype(np.float32)
    high = full.astype(BF16)
    low = (full - high.astype(np.float32)).astype(BF16)
    return high, low


def lag_table():
    shifts = np.arange(LAGS) - LAGS // 2
    angle = 2.0 * np.pi / SAMPLES * (((BAND_START + BIN_ORDER)[None, :] * shifts[:, None]) % SAMPLES)
    return np.concatenate([np.cos(angle), -np.sin(angle)], axis=1).astype(np.float32).astype(BF16)


def window_tables():
    near = np.abs(BIN_ORDER[:, None] - BIN_ORDER[None, :]) <= HALF
    count = near.sum(axis=1).astype(np.float32)
    return near.astype(BF16), np.ascontiguousarray(np.broadcast_to(count[:, None], (FREQS, 256)))


def split(value):
    high = value.astype(jnp.bfloat16)
    return high, (value - high.astype(jnp.float32)).astype(jnp.bfloat16)


def dot_nt(a, b):
    return lax.dot_general(a, b, (((1,), (1,)), ((), ())), preferred_element_type=jnp.float32)


def dot_nn(a, b):
    return jnp.dot(a, b, preferred_element_type=jnp.float32)


def whiten_kernel(*refs):
    xs = refs[:RADIX]
    high_ref, low_ref, near_ref, count_ref, perm_ref, out_ref, total = refs[RADIX:]
    step = pl.program_id(0)

    @pl.when(step == 0)
    def _():
        total[...] = jnp.zeros_like(total)

    x = [ref[...].astype(jnp.float32) for ref in xs]
    e0, e1, e2, e3 = x[0] + x[4], x[1] + x[5], x[2] + x[6], x[3] + x[7]
    d0, d1, d2, d3 = x[0] - x[4], x[1] - x[5], x[2] - x[6], x[3] - x[7]
    root = math.sqrt(0.5)
    plus, minus = (d1 + d3) * root, (d1 - d3) * root
    folded = (
        ((e0 + e2) + (e1 + e3), (e0 + e2) - (e1 + e3)),
        (d0 + minus, -(d2 + plus)),
        (e0 - e2, e3 - e1),
        (d0 - minus, d2 - plus),
    )
    for group, (a, b) in enumerate(folded):
        a_high, a_low = split(a)
        b_high, b_low = split(b)
        y_high = jnp.concatenate([a_high, b_high], axis=1)
        y_low = jnp.concatenate([a_low, b_low], axis=1)
        t_high = high_ref[0, group]
        part = dot_nt(t_high, y_high) + dot_nt(t_high, y_low) + dot_nt(low_ref[0, group], y_high)
        total[group] += part

    @pl.when(step == STEPS - 1)
    def _():
        real, imag = [], []
        for group in range(4):
            for half in range(2):
                base = half * 2 * PER_RES
                real.append(total[group, base:base + PER_RES])
                imag.append(total[group, base + PER_RES:base + 2 * PER_RES])
        real = jnp.concatenate(real, axis=0)
        imag = jnp.concatenate(imag, axis=0)
        amplitude = jnp.sqrt(real * real + imag * imag)
        high, rest = amplitude.astype(jnp.bfloat16), None
        rest = amplitude - high.astype(jnp.float32)
        mid, low = split(rest)
        near = near_ref[...]
        summed = dot_nn(near, high) + (dot_nn(near, mid) + dot_nn(near, low))
        divisor = jnp.maximum(summed / count_ref[...], 1.0)
        segs = out_ref.shape[0]
        for part, value in enumerate((real, imag)):
            white = (value / divisor).astype(jnp.bfloat16)
            moved = dot_nn(white, perm_ref[...]).astype(jnp.bfloat16)
            width = moved.shape[1] // segs
            for s in range(segs):
                out_ref[s, part] = moved[:, s * width:(s + 1) * width]


def whiten(signal, block_size, segs):
    rows = block_size * segs
    high, low = dft_tables()
    near, count = window_tables()
    perm = np.zeros((rows, rows), np.float32)
    for c in range(block_size):
        for s in range(segs):
            perm[c * segs + s, s * block_size + c] = 1.0
    once = lambda shape: pl.BlockSpec(shape, lambda q: (0,) * len(shape))
    table = pl.BlockSpec((1, 4, 4 * PER_RES, 2 * CHUNK), lambda q: (q, 0, 0, 0))
    return pl.pallas_call(
        whiten_kernel,
        grid=(STEPS,),
        in_specs=[
            pl.BlockSpec((rows, CHUNK), functools.partial(lambda j, q: (0, j * STEPS + q), j))
            for j in range(RADIX)
        ] + [table, table, once((FREQS, FREQS)), once((FREQS, 256)), once((rows, rows))],
        out_specs=once((segs, 2, FREQS, block_size)),
        out_shape=jax.ShapeDtypeStruct((segs, 2, FREQS, block_size), jnp.bfloat16),
        scratch_shapes=[pltpu.VMEM((4, 4 * PER_RES, rows), jnp.float32)],
        compiler_params=pltpu.CompilerParams(vmem_limit_bytes=48 << 20),
    )(*([signal] * RADIX), jnp.asarray(high), jnp.asarray(low), jnp.asarray(near),
      jnp.asarray(count[:, :rows]), jnp.asarray(perm.astype(BF16)))


PLANES = 4
MESH = pl.DeviceIdType.MESH


def gather_kernel(own_ref, all_ref, z_send, z_recv, p_send, p_recv, c_send, c_recv, own_sem):
    chan, seg = lax.axis_index("chan"), lax.axis_index("seg")
    y, x, core = chan // 4, (chan // 2) % 2, chan % 2
    x_near = 4 * y + 2 * (1 - x) + core
    y_near = 4 * (1 - y) + 2 * x + core
    across = 4 * (1 - y) + 2 * (1 - x) + core
    twin = 4 * y + 2 * x + (1 - core)

    barrier = pltpu.get_barrier_semaphore()
    for other in (x_near, y_near, twin):
        pl.semaphore_signal(barrier, inc=1, device_id=(other, seg), device_id_type=MESH)

    def send(src, dst, send_sem, recv_sem, device):
        copy = pltpu.make_async_remote_copy(
            src_ref=src, dst_ref=dst, send_sem=send_sem, recv_sem=recv_sem,
            device_id=device, device_id_type=MESH,
        )
        copy.start()
        return copy

    def program(z):
        for step in (1, -1):
            if 0 <= z + step < PLANES:
                pl.semaphore_signal(barrier, inc=1, device_id=(chan, z + step), device_id_type=MESH)
        pl.semaphore_wait(barrier, 3 + (z > 0) + (z < PLANES - 1))
        sent = []
        order = sorted(range(PLANES), key=lambda other: abs(other - z))
        local = pltpu.make_async_copy(own_ref, all_ref.at[chan, z], own_sem)
        local.start()

        def piece(other):
            return own_ref if other == z else all_ref.at[chan, other]

        def along(other):
            for step, side in ((1, 0), (-1, 1)):
                away = other == z or (z - other) * step > 0
                if away and 0 <= z + step < PLANES:
                    sent.append(send(piece(other), all_ref.at[chan, other], z_send.at[other, side],
                                     z_recv.at[other], (chan, z + step)))

        def landed(ref, sem):
            pltpu.make_async_remote_copy(
                src_ref=ref, dst_ref=ref, send_sem=sem, recv_sem=sem,
                device_id=(twin, z), device_id_type=MESH,
            ).wait_recv()

        def to_twin(src, block, other, half, slot):
            sent.append(send(src, all_ref.at[block, other, half], c_send.at[other, slot, half],
                             c_recv.at[other, slot, half], (twin, z)))

        def outward(other):
            for half in (0, 1):
                for way, near in ((0, x_near), (1, y_near)):
                    part = half if way == 0 else 1 - half
                    sent.append(send(piece(other).at[part], all_ref.at[chan, other, part],
                                     p_send.at[other, way, part], p_recv.at[other, way, part], (near, z)))
            for half in (0, 1):
                to_twin(piece(other).at[half], chan, other, half, 0)

        def onward(other):
            for first in (0, 1):
                for way, block in ((0, x_near), (1, y_near)):
                    half = first if way == 0 else 1 - first
                    ref = all_ref.at[block, other, half]
                    landed(ref, p_recv.at[other, way, half])
                    if half == way:
                        sent.append(send(ref, ref, p_send.at[other, 2, half], p_recv.at[other, 2, half],
                                         ((y_near, x_near)[way], z)))
                    to_twin(ref, block, other, half, 1 + way)

        def finish(other):
            for half in (0, 1):
                ref = all_ref.at[across, other, half]
                landed(ref, p_recv.at[other, 2, half])
                to_twin(ref, across, other, half, 3)

        along(z)
        outward(z)
        for k in range(1, PLANES):
            landed(all_ref.at[chan, order[k]], z_recv.at[order[k]])
            along(order[k])
            outward(order[k])
            onward(order[k - 1])
            if k > 1:
                finish(order[k - 2])
        onward(order[-1])
        finish(order[-2])
        finish(order[-1])
        twin_blocks = [4 * y + 2 * x, 4 * y + 2 * (1 - x), 4 * (1 - y) + 2 * x, 4 * (1 - y) + 2 * (1 - x)]
        for other in range(PLANES):
            for slot, block in enumerate(twin_blocks):
                for half in (0, 1):
                    landed(all_ref.at[block + 1 - core, other, half], c_recv.at[other, slot, half])
        for copy in sent:
            copy.wait_send()
        local.wait()

    for z in range(PLANES):
        pl.when(seg == z)(functools.partial(program, z))


def gather(own):
    dma = pltpu.SemaphoreType.DMA
    return pl.pallas_call(
        gather_kernel,
        in_specs=[pl.BlockSpec(memory_space=pl.ANY)],
        out_specs=pl.BlockSpec(memory_space=pl.ANY),
        out_shape=jax.ShapeDtypeStruct((8, PLANES) + own.shape, own.dtype),
        scratch_shapes=[
            dma((PLANES, 2)), dma((PLANES,)),
            dma((PLANES, 3, 2)), dma((PLANES, 3, 2)),
            dma((PLANES, 4, 2)), dma((PLANES, 4, 2)), dma,
        ],
        compiler_params=pltpu.CompilerParams(collective_id=0, has_side_effects=True),
    )(own)


GROUP = 16
FCHUNK = 128
CROSS_STEPS = FREQS // FCHUNK
ROWS_STEP = 8


def stack_kernel(norm_factor, parts, segs, rows, index_ref, first_ref, second_ref, table_ref, out_ref, cross):
    step = pl.program_id(1)
    depth = parts * segs * 2 * GROUP
    block = second_ref.shape[-1]

    @pl.when(step < CROSS_STEPS)
    def _():
        own = index_ref[4] * rows
        select = (
            lax.broadcasted_iota(jnp.int32, (rows, block), 1)
            == lax.broadcasted_iota(jnp.int32, (rows, block), 0) + own
        ).astype(jnp.bfloat16)
        mask = (
            lax.broadcasted_iota(jnp.int32, (rows, GROUP, depth), 2) % GROUP
            == lax.broadcasted_iota(jnp.int32, (rows, GROUP, depth), 1)
        )
        for g in range(FCHUNK // GROUP):
            span = slice(g * GROUP, (g + 1) * GROUP)
            firsts, plain, turned = [], [], []
            for z in range(parts):
                for s in range(segs):
                    firsts += [first_ref[0, z, s, p, span] for p in range(2)]
                    re, im = second_ref[0, z, s, 0, span], second_ref[0, z, s, 1, span]
                    plain += [re, im]
                    turned += [-im, re]
            left = dot_nt(select, jnp.concatenate(firsts, axis=0))
            wide = jnp.broadcast_to(left[:, None, :], (rows, GROUP, depth))
            wide = jnp.where(mask, wide, 0.0).reshape(rows * GROUP, depth).astype(jnp.bfloat16)
            right = jnp.concatenate(
                [jnp.concatenate(plain, axis=0), jnp.concatenate(turned, axis=0)], axis=1
            )
            result = dot_nn(wide, right).astype(jnp.bfloat16).reshape(rows, GROUP, 2 * block)
            at = pl.multiple_of(step * FCHUNK + g * GROUP, GROUP)
            cross[:, 0, pl.ds(at, GROUP), :] = result[:, :, :block]
            cross[:, 1, pl.ds(at, GROUP), :] = result[:, :, block:]

    @pl.when(step >= CROSS_STEPS)
    def _():
        base = (step - CROSS_STEPS) * ROWS_STEP
        table = table_ref[...]
        for pair in range(ROWS_STEP // 2):
            both = [
                cross[base + 2 * pair + h].reshape(2 * FREQS, block) for h in range(2)
            ]
            lagged = dot_nn(table, jnp.concatenate(both, axis=1)) * norm_factor
            for h in range(2):
                out_ref[2 * pair + h, 0] = lagged[:, h * block:(h + 1) * block].T


def stack(index, gathered, norm_factor, rows):
    _, parts, segs, _, _, block = gathered.shape
    grid = (TILE_DEV, CROSS_STEPS + rows // ROWS_STEP)
    shape = (1, parts, segs, 2, FCHUNK, block)

    def place(offset, slot, step, index_ref):
        return (index_ref[offset + slot], 0, 0, 0, jnp.minimum(step, CROSS_STEPS - 1), 0)

    return pl.pallas_call(
        functools.partial(stack_kernel, norm_factor, parts, segs, rows),
        grid_spec=pltpu.PrefetchScalarGridSpec(
            num_scalar_prefetch=1,
            grid=grid,
            in_specs=[
                pl.BlockSpec(shape, functools.partial(place, 0)),
                pl.BlockSpec(shape, functools.partial(place, TILE_DEV)),
                pl.BlockSpec((LAGS, 2 * FREQS), lambda slot, step, index_ref: (0, 0)),
            ],
            out_specs=pl.BlockSpec(
                (ROWS_STEP, 1, block, LAGS),
                lambda slot, step, index_ref: (jnp.maximum(step - CROSS_STEPS, 0), slot, 0, 0),
            ),
            scratch_shapes=[pltpu.VMEM((rows, 2, FREQS, block), jnp.bfloat16)],
        ),
        out_shape=jax.ShapeDtypeStruct((rows, TILE_DEV, block, LAGS), jnp.float32),
        compiler_params=pltpu.CompilerParams(vmem_limit_bytes=48 << 20),
    )(index, gathered, gathered, jnp.asarray(lag_table()))


def pair_blocks(pair_offsets, pair_counts, pair_owner, block_count, slot_count):
    slot_index = lax.iota(jnp.int32, slot_count)
    starts = jnp.cumsum(pair_counts) - pair_counts
    first_block = jnp.sum((starts[None, :] <= slot_index[:, None]).astype(jnp.int32), axis=1) - 1
    member = lax.iota(jnp.int32, block_count)[None, :] == first_block[:, None]
    start_of = jnp.sum(jnp.where(member, starts[None, :], 0), axis=1)
    position = slot_index - start_of
    listed = jnp.sum(jnp.where(member[:, :, None], pair_offsets[None, :, :], 0), axis=1)
    chosen = lax.iota(jnp.int32, pair_offsets.shape[1])[None, :] == position[:, None]
    offset = jnp.sum(jnp.where(chosen, listed, 0), axis=1)
    second_block = jnp.mod(first_block + offset, block_count)
    held = pair_owner[None, :] == slot_index[:, None]
    slot_first = jnp.sum(jnp.where(held, first_block[None, :], 0), axis=1)
    slot_second = jnp.sum(jnp.where(held, second_block[None, :], 0), axis=1)
    return (slot_first, slot_second)


def on_device(traces, pair_offsets, pair_counts, pair_owner):
    block_size, local_segs, sample_count = traces.shape
    parts_count = lax.axis_size("seg")
    block_count = lax.axis_size("chan")
    norm_factor = 1.0 / math.sqrt(FREQS * local_segs * parts_count)
    signal = traces.reshape(block_size * local_segs, sample_count)
    whitened = whiten(signal, block_size, local_segs)
    if (block_count, parts_count) == (8, PLANES):
        gathered = gather(whitened)
    else:
        gathered = lax.all_gather(lax.all_gather(whitened, "seg", axis=0), "chan", axis=0)
    slot_first, slot_second = pair_blocks(
        pair_offsets, pair_counts, pair_owner, block_count, pair_owner.shape[0]
    )
    my_start = lax.axis_index("chan") * TILE_DEV
    index = jnp.concatenate(
        [
            lax.dynamic_slice_in_dim(slot_first, my_start, TILE_DEV),
            lax.dynamic_slice_in_dim(slot_second, my_start, TILE_DEV),
            lax.axis_index("seg")[None],
        ]
    ).astype(jnp.int32)
    return stack(index, gathered, norm_factor, block_size // parts_count)


def solution(mesh):
    placed = (P("chan", "seg", None), P(), P(), P())
    return jax.shard_map(
        on_device,
        mesh=mesh,
        in_specs=placed,
        out_specs=P("seg", "chan", None, None),
        check_vma=False,
    )
```

```python
import functools
import math

import jax
import jax.numpy as jnp
import ml_dtypes
import numpy as np
from jax import lax
from jax.experimental import pallas as pl
from jax.experimental.pallas import tpu as pltpu
from jax.sharding import PartitionSpec as P

SAMPLES = 8192
BAND_START = 32
FREQS = 512
HALF = 8
LAGS = 256
TILE_DEV = 2

RADIX = 8
FOLDED = SAMPLES // RADIX
RESIDUES = (0, 4, 1, 7, 2, 6, 3, 5)
PER_RES = FREQS // RADIX
CHUNK = 256
STEPS = FOLDED // CHUNK
BF16 = ml_dtypes.bfloat16

BIN_ORDER = np.concatenate([np.arange(PER_RES) * RADIX + r for r in RESIDUES])


def dft_tables():
    n = np.arange(FOLDED)
    full = np.zeros((4, 4 * PER_RES, 2, FOLDED))
    for group in range(4):
        first, second = RESIDUES[2 * group], RESIDUES[2 * group + 1]
        parts = []
        for r in (first, second):
            k = BAND_START + np.arange(PER_RES) * RADIX + r
            angle = 2.0 * np.pi / SAMPLES * ((k[:, None] * n[None, :]) % SAMPLES)
            parts.append((np.cos(angle), np.sin(angle)))
        (c0, s0), (c1, s1) = parts
        o = np.zeros_like(c0)
        if group == 0:
            rows = [(c0, o), (-s0, o), (o, c1), (o, -s1)]
        else:
            rows = [(c0, s0), (-s0, c0), (c1, -s1), (-s1, -c1)]
        for i, (a, b) in enumerate(rows):
            full[group, i * PER_RES:(i + 1) * PER_RES, 0] = a
            full[group, i * PER_RES:(i + 1) * PER_RES, 1] = b
    full = full.reshape(4, 4 * PER_RES, 2, STEPS, CHUNK).transpose(3, 0, 1, 2, 4)
    full = full.reshape(STEPS, 4, 4 * PER_RES, 2 * CHUNK).astype(np.float32)
    high = full.astype(BF16)
    low = (full - high.astype(np.float32)).astype(BF16)
    return high, low


def lag_table():
    shifts = np.arange(LAGS) - LAGS // 2
    angle = 2.0 * np.pi / SAMPLES * (((BAND_START + BIN_ORDER)[None, :] * shifts[:, None]) % SAMPLES)
    return np.concatenate([np.cos(angle), -np.sin(angle)], axis=1).astype(np.float32).astype(BF16)


def window_tables():
    near = np.abs(BIN_ORDER[:, None] - BIN_ORDER[None, :]) <= HALF
    count = near.sum(axis=1).astype(np.float32)
    return near.astype(BF16), np.ascontiguousarray(np.broadcast_to(count[:, None], (FREQS, 256)))


def split(value):
    high = value.astype(jnp.bfloat16)
    return high, (value - high.astype(jnp.float32)).astype(jnp.bfloat16)


def dot_nt(a, b):
    return lax.dot_general(a, b, (((1,), (1,)), ((), ())), preferred_element_type=jnp.float32)


def dot_nn(a, b):
    return jnp.dot(a, b, preferred_element_type=jnp.float32)


def whiten_kernel(*refs):
    xs = refs[:RADIX]
    high_ref, low_ref, near_ref, count_ref, perm_ref, out_ref, total = refs[RADIX:]
    step = pl.program_id(0)

    @pl.when(step == 0)
    def _():
        total[...] = jnp.zeros_like(total)

    x = [ref[...].astype(jnp.float32) for ref in xs]
    e0, e1, e2, e3 = x[0] + x[4], x[1] + x[5], x[2] + x[6], x[3] + x[7]
    d0, d1, d2, d3 = x[0] - x[4], x[1] - x[5], x[2] - x[6], x[3] - x[7]
    root = math.sqrt(0.5)
    plus, minus = (d1 + d3) * root, (d1 - d3) * root
    folded = (
        ((e0 + e2) + (e1 + e3), (e0 + e2) - (e1 + e3)),
        (d0 + minus, -(d2 + plus)),
        (e0 - e2, e3 - e1),
        (d0 - minus, d2 - plus),
    )
    for group, (a, b) in enumerate(folded):
        a_high, a_low = split(a)
        b_high, b_low = split(b)
        y_high = jnp.concatenate([a_high, b_high], axis=1)
        y_low = jnp.concatenate([a_low, b_low], axis=1)
        t_high = high_ref[0, group]
        part = dot_nt(t_high, y_high) + dot_nt(t_high, y_low) + dot_nt(low_ref[0, group], y_high)
        total[group] += part

    @pl.when(step == STEPS - 1)
    def _():
        real, imag = [], []
        for group in range(4):
            for half in range(2):
                base = half * 2 * PER_RES
                real.append(total[group, base:base + PER_RES])
                imag.append(total[group, base + PER_RES:base + 2 * PER_RES])
        real = jnp.concatenate(real, axis=0)
        imag = jnp.concatenate(imag, axis=0)
        amplitude = jnp.sqrt(real * real + imag * imag)
        high, rest = amplitude.astype(jnp.bfloat16), None
        rest = amplitude - high.astype(jnp.float32)
        mid, low = split(rest)
        near = near_ref[...]
        summed = dot_nn(near, high) + (dot_nn(near, mid) + dot_nn(near, low))
        divisor = jnp.maximum(summed / count_ref[...], 1.0)
        segs = out_ref.shape[0]
        for part, value in enumerate((real, imag)):
            white = (value / divisor).astype(jnp.bfloat16)
            moved = dot_nn(white, perm_ref[...]).astype(jnp.bfloat16)
            width = moved.shape[1] // segs
            for s in range(segs):
                out_ref[s, part] = moved[:, s * width:(s + 1) * width]


def whiten(signal, block_size, segs):
    rows = block_size * segs
    high, low = dft_tables()
    near, count = window_tables()
    perm = np.zeros((rows, rows), np.float32)
    for c in range(block_size):
        for s in range(segs):
            perm[c * segs + s, s * block_size + c] = 1.0
    once = lambda shape: pl.BlockSpec(shape, lambda q: (0,) * len(shape))
    table = pl.BlockSpec((1, 4, 4 * PER_RES, 2 * CHUNK), lambda q: (q, 0, 0, 0))
    return pl.pallas_call(
        whiten_kernel,
        grid=(STEPS,),
        in_specs=[
            pl.BlockSpec((rows, CHUNK), functools.partial(lambda j, q: (0, j * STEPS + q), j))
            for j in range(RADIX)
        ] + [table, table, once((FREQS, FREQS)), once((FREQS, 256)), once((rows, rows))],
        out_specs=once((segs, 2, FREQS, block_size)),
        out_shape=jax.ShapeDtypeStruct((segs, 2, FREQS, block_size), jnp.bfloat16),
        scratch_shapes=[pltpu.VMEM((4, 4 * PER_RES, rows), jnp.float32)],
        compiler_params=pltpu.CompilerParams(vmem_limit_bytes=48 << 20),
    )(*([signal] * RADIX), jnp.asarray(high), jnp.asarray(low), jnp.asarray(near),
      jnp.asarray(count[:, :rows]), jnp.asarray(perm.astype(BF16)))


PLANES = 4
MESH = pl.DeviceIdType.MESH
LINE_ROWS = 1536


def gather_kernel(own_ref, all_ref, z_send, z_recv, p_send, p_recv, c_send, c_recv,
                  bz_send, bz_recv, bp_send, bp_recv, bc_send, bc_recv, own_sem):
    chan, seg = lax.axis_index("chan"), lax.axis_index("seg")
    y, x, core = chan // 4, (chan // 2) % 2, chan % 2
    x_near = 4 * y + 2 * (1 - x) + core
    y_near = 4 * (1 - y) + 2 * x + core
    across = 4 * (1 - y) + 2 * (1 - x) + core
    twin = 4 * y + 2 * x + (1 - core)
    blocks = (chan, x_near, y_near, across)
    twin_blocks = [block + 1 - 2 * core for block in blocks]
    near = (x_near, y_near)
    total_rows = own_ref.shape[0]
    line = pl.ds(0, LINE_ROWS)
    line_half = [pl.ds(h * (LINE_ROWS // 2), LINE_ROWS // 2) for h in (0, 1)]
    rest_rows = total_rows - LINE_ROWS
    rest = pl.ds(LINE_ROWS, rest_rows)
    rest_half = [pl.ds(LINE_ROWS + h * (rest_rows // 2), rest_rows // 2) for h in (0, 1)]

    barrier = pltpu.get_barrier_semaphore()
    for other in (x_near, y_near, twin):
        pl.semaphore_signal(barrier, inc=1, device_id=(other, seg), device_id_type=MESH)

    def program(z):
        for step in (1, -1):
            if 0 <= z + step < PLANES:
                pl.semaphore_signal(barrier, inc=1, device_id=(chan, z + step), device_id_type=MESH)
        pl.semaphore_wait(barrier, 3 + int(z > 0) + int(z < PLANES - 1))
        sent = []
        order = sorted(range(PLANES), key=lambda other: abs(other - z))

        def send(src, dst, send_sem, recv_sem, device):
            copy = pltpu.make_async_remote_copy(
                src_ref=src, dst_ref=dst, send_sem=send_sem, recv_sem=recv_sem,
                device_id=device, device_id_type=MESH,
            )
            copy.start()
            sent.append(copy)

        def landed(ref, sem):
            pltpu.make_async_remote_copy(
                src_ref=ref, dst_ref=ref, send_sem=sem, recv_sem=sem,
                device_id=(twin, z), device_id_type=MESH,
            ).wait_recv()

        def part(block, other, rows):
            if block == 0 and other == z:
                return own_ref.at[rows]
            return all_ref.at[blocks[block], other, rows]

        def along(block, other, rows, send_sem, recv_sem):
            for step, side in ((1, 0), (-1, 1)):
                away = other == z or (z - other) * step > 0
                if away and 0 <= z + step < PLANES:
                    send(part(block, other, rows), all_ref.at[blocks[block], other, rows],
                         send_sem.at[other, block, side], recv_sem.at[other, block], (chan, z + step))

        def to_twin(block, other, rows, send_sem, recv_sem, half):
            send(part(block, other, rows), all_ref.at[blocks[block], other, rows],
                 send_sem.at[other, block, half], recv_sem.at[other, block, half], (twin, z))

        def outward(other, halves, send_sem, recv_sem):
            for first in (0, 1):
                for way in (0, 1):
                    half = first if way == 0 else 1 - first
                    send(part(0, other, halves[half]), all_ref.at[chan, other, halves[half]],
                         send_sem.at[other, way, half], recv_sem.at[other, way, half], (near[way], z))

        def onward(other, halves, send_sem, recv_sem, first):
            for way in (0, 1):
                half = first if way == 0 else 1 - first
                ref = all_ref.at[near[way], other, halves[half]]
                landed(ref, recv_sem.at[other, way, half])
                if half == way:
                    send(ref, ref, send_sem.at[other, 2, half], recv_sem.at[other, 2, half],
                         (near[1 - way], z))

        def finish(other, halves, recv_sem):
            for half in (0, 1):
                landed(all_ref.at[across, other, halves[half]], recv_sem.at[other, 2, half])

        def line_out(other):
            outward(other, line_half, p_send, p_recv)
            for half in (0, 1):
                to_twin(0, other, line_half[half], c_send, c_recv, half)

        def line_on(other):
            for first in (0, 1):
                onward(other, line_half, p_send, p_recv, first)
                to_twin(1, other, line_half[first], c_send, c_recv, first)
                to_twin(2, other, line_half[1 - first], c_send, c_recv, 1 - first)

        def line_finish(other):
            finish(other, line_half, p_recv)
            for half in (0, 1):
                to_twin(3, other, line_half[half], c_send, c_recv, half)

        def rest_line(other):
            for block in range(4):
                landed(all_ref.at[blocks[block], other, rest], bz_recv.at[other, block])
                along(block, other, rest, bz_send, bz_recv)
                to_twin(block, other, rest, bc_send, bc_recv, 0)

        along(0, z, line, z_send, z_recv)
        outward(z, rest_half, bp_send, bp_recv)
        along(0, z, rest, bz_send, bz_recv)
        to_twin(0, z, rest, bc_send, bc_recv, 0)
        local = pltpu.make_async_copy(own_ref, all_ref.at[chan, z], own_sem)
        local.start()
        line_out(z)
        for first in (0, 1):
            onward(z, rest_half, bp_send, bp_recv, first)
        for block in (1, 2):
            along(block, z, rest, bz_send, bz_recv)
            to_twin(block, z, rest, bc_send, bc_recv, 0)
        finish(z, rest_half, bp_recv)
        along(3, z, rest, bz_send, bz_recv)
        to_twin(3, z, rest, bc_send, bc_recv, 0)
        for k in range(1, PLANES):
            landed(all_ref.at[chan, order[k], line], z_recv.at[order[k], 0])
            along(0, order[k], line, z_send, z_recv)
            line_out(order[k])
            line_on(order[k - 1])
            rest_line(order[k])
            if k > 1:
                line_finish(order[k - 2])
        line_on(order[-1])
        line_finish(order[-2])
        line_finish(order[-1])
        for other in range(PLANES):
            for block in range(4):
                ref = all_ref.at[twin_blocks[block], other]
                for half in (0, 1):
                    landed(ref.at[line_half[half]], c_recv.at[other, block, half])
                landed(ref.at[rest], bc_recv.at[other, block, 0])
        for copy in sent:
            copy.wait_send()
        local.wait()

    for z in range(PLANES):
        pl.when(seg == z)(functools.partial(program, z))


def gather(own):
    dma = pltpu.SemaphoreType.DMA
    rows, lanes = math.prod(own.shape[:-1]), own.shape[-1]
    gathered = pl.pallas_call(
        gather_kernel,
        in_specs=[pl.BlockSpec(memory_space=pl.ANY)],
        out_specs=pl.BlockSpec(memory_space=pl.ANY),
        out_shape=jax.ShapeDtypeStruct((8, PLANES, rows, lanes), own.dtype),
        scratch_shapes=[
            dma((PLANES, 1, 2)), dma((PLANES, 1)),
            dma((PLANES, 3, 2)), dma((PLANES, 3, 2)),
            dma((PLANES, 4, 2)), dma((PLANES, 4, 2)),
            dma((PLANES, 4, 2)), dma((PLANES, 4)),
            dma((PLANES, 3, 2)), dma((PLANES, 3, 2)),
            dma((PLANES, 4, 1)), dma((PLANES, 4, 1)), dma,
        ],
        compiler_params=pltpu.CompilerParams(collective_id=0, has_side_effects=True),
    )(own.reshape(rows, lanes))
    return gathered.reshape((8, PLANES) + own.shape)


GROUP = 16
FCHUNK = 128
CROSS_STEPS = FREQS // FCHUNK
ROWS_STEP = 8


def stack_kernel(norm_factor, parts, segs, rows, index_ref, first_ref, second_ref, table_ref, out_ref, cross):
    step = pl.program_id(1)
    depth = parts * segs * 2 * GROUP
    block = second_ref.shape[-1]

    @pl.when(step < CROSS_STEPS)
    def _():
        own = index_ref[4] * rows
        select = (
            lax.broadcasted_iota(jnp.int32, (rows, block), 1)
            == lax.broadcasted_iota(jnp.int32, (rows, block), 0) + own
        ).astype(jnp.bfloat16)
        mask = (
            lax.broadcasted_iota(jnp.int32, (rows, GROUP, depth), 2) % GROUP
            == lax.broadcasted_iota(jnp.int32, (rows, GROUP, depth), 1)
        )
        for g in range(FCHUNK // GROUP):
            span = slice(g * GROUP, (g + 1) * GROUP)
            firsts, plain, turned = [], [], []
            for z in range(parts):
                for s in range(segs):
                    firsts += [first_ref[0, z, s, p, span] for p in range(2)]
                    re, im = second_ref[0, z, s, 0, span], second_ref[0, z, s, 1, span]
                    plain += [re, im]
                    turned += [-im, re]
            left = dot_nt(select, jnp.concatenate(firsts, axis=0))
            wide = jnp.broadcast_to(left[:, None, :], (rows, GROUP, depth))
            wide = jnp.where(mask, wide, 0.0).reshape(rows * GROUP, depth).astype(jnp.bfloat16)
            right = jnp.concatenate(
                [jnp.concatenate(plain, axis=0), jnp.concatenate(turned, axis=0)], axis=1
            )
            result = dot_nn(wide, right).astype(jnp.bfloat16).reshape(rows, GROUP, 2 * block)
            at = pl.multiple_of(step * FCHUNK + g * GROUP, GROUP)
            cross[:, 0, pl.ds(at, GROUP), :] = result[:, :, :block]
            cross[:, 1, pl.ds(at, GROUP), :] = result[:, :, block:]

    @pl.when(step >= CROSS_STEPS)
    def _():
        base = (step - CROSS_STEPS) * ROWS_STEP
        table = table_ref[...]
        for pair in range(ROWS_STEP // 2):
            both = [
                cross[base + 2 * pair + h].reshape(2 * FREQS, block) for h in range(2)
            ]
            lagged = dot_nn(table, jnp.concatenate(both, axis=1)) * norm_factor
            for h in range(2):
                out_ref[2 * pair + h, 0] = lagged[:, h * block:(h + 1) * block].T


def stack(index, gathered, norm_factor, rows):
    _, parts, segs, _, _, block = gathered.shape
    grid = (TILE_DEV, CROSS_STEPS + rows // ROWS_STEP)
    shape = (1, parts, segs, 2, FCHUNK, block)

    def place(offset, slot, step, index_ref):
        return (index_ref[offset + slot], 0, 0, 0, jnp.minimum(step, CROSS_STEPS - 1), 0)

    return pl.pallas_call(
        functools.partial(stack_kernel, norm_factor, parts, segs, rows),
        grid_spec=pltpu.PrefetchScalarGridSpec(
            num_scalar_prefetch=1,
            grid=grid,
            in_specs=[
                pl.BlockSpec(shape, functools.partial(place, 0)),
                pl.BlockSpec(shape, functools.partial(place, TILE_DEV)),
                pl.BlockSpec((LAGS, 2 * FREQS), lambda slot, step, index_ref: (0, 0)),
            ],
            out_specs=pl.BlockSpec(
                (ROWS_STEP, 1, block, LAGS),
                lambda slot, step, index_ref: (jnp.maximum(step - CROSS_STEPS, 0), slot, 0, 0),
            ),
            scratch_shapes=[pltpu.VMEM((rows, 2, FREQS, block), jnp.bfloat16)],
        ),
        out_shape=jax.ShapeDtypeStruct((rows, TILE_DEV, block, LAGS), jnp.float32),
        compiler_params=pltpu.CompilerParams(vmem_limit_bytes=48 << 20),
    )(index, gathered, gathered, jnp.asarray(lag_table()))


def pair_blocks(pair_offsets, pair_counts, pair_owner, block_count, slot_count):
    slot_index = lax.iota(jnp.int32, slot_count)
    starts = jnp.cumsum(pair_counts) - pair_counts
    first_block = jnp.sum((starts[None, :] <= slot_index[:, None]).astype(jnp.int32), axis=1) - 1
    member = lax.iota(jnp.int32, block_count)[None, :] == first_block[:, None]
    start_of = jnp.sum(jnp.where(member, starts[None, :], 0), axis=1)
    position = slot_index - start_of
    listed = jnp.sum(jnp.where(member[:, :, None], pair_offsets[None, :, :], 0), axis=1)
    chosen = lax.iota(jnp.int32, pair_offsets.shape[1])[None, :] == position[:, None]
    offset = jnp.sum(jnp.where(chosen, listed, 0), axis=1)
    second_block = jnp.mod(first_block + offset, block_count)
    held = pair_owner[None, :] == slot_index[:, None]
    slot_first = jnp.sum(jnp.where(held, first_block[None, :], 0), axis=1)
    slot_second = jnp.sum(jnp.where(held, second_block[None, :], 0), axis=1)
    return (slot_first, slot_second)


def on_device(traces, pair_offsets, pair_counts, pair_owner):
    block_size, local_segs, sample_count = traces.shape
    parts_count = lax.axis_size("seg")
    block_count = lax.axis_size("chan")
    norm_factor = 1.0 / math.sqrt(FREQS * local_segs * parts_count)
    signal = traces.reshape(block_size * local_segs, sample_count)
    whitened = whiten(signal, block_size, local_segs)
    if (block_count, parts_count) == (8, PLANES):
        gathered = gather(whitened)
    else:
        gathered = lax.all_gather(lax.all_gather(whitened, "seg", axis=0), "chan", axis=0)
    slot_first, slot_second = pair_blocks(
        pair_offsets, pair_counts, pair_owner, block_count, pair_owner.shape[0]
    )
    my_start = lax.axis_index("chan") * TILE_DEV
    index = jnp.concatenate(
        [
            lax.dynamic_slice_in_dim(slot_first, my_start, TILE_DEV),
            lax.dynamic_slice_in_dim(slot_second, my_start, TILE_DEV),
            lax.axis_index("seg")[None],
        ]
    ).astype(jnp.int32)
    return stack(index, gathered, norm_factor, block_size // parts_count)


def solution(mesh):
    placed = (P("chan", "seg", None), P(), P(), P())
    return jax.shard_map(
        on_device,
        mesh=mesh,
        in_specs=placed,
        out_specs=P("seg", "chan", None, None),
        check_vma=False,
    )
```

```python
import functools
import math

import jax
import jax.numpy as jnp
import ml_dtypes
import numpy as np
from jax import lax
from jax.experimental import pallas as pl
from jax.experimental.pallas import tpu as pltpu
from jax.sharding import PartitionSpec as P

SAMPLES = 8192
BAND_START = 32
FREQS = 512
HALF = 8
LAGS = 256
TILE_DEV = 2

RADIX = 8
FOLDED = SAMPLES // RADIX
RESIDUES = (0, 4, 1, 7, 2, 6, 3, 5)
PER_RES = FREQS // RADIX
LANES = 128
PARTS = FOLDED // LANES
BF16 = ml_dtypes.bfloat16

BIN_ORDER = np.concatenate([np.arange(PER_RES) * RADIX + r for r in RESIDUES])


def dft_tables():
    n = np.arange(FOLDED)
    full = np.zeros((4, 4 * PER_RES, 2, FOLDED))
    for group in range(4):
        first, second = RESIDUES[2 * group], RESIDUES[2 * group + 1]
        parts = []
        for r in (first, second):
            k = BAND_START + np.arange(PER_RES) * RADIX + r
            angle = 2.0 * np.pi / SAMPLES * ((k[:, None] * n[None, :]) % SAMPLES)
            parts.append((np.cos(angle), np.sin(angle)))
        (c0, s0), (c1, s1) = parts
        o = np.zeros_like(c0)
        if group == 0:
            rows = [(c0, o), (-s0, o), (o, c1), (o, -s1)]
        else:
            rows = [(c0, s0), (-s0, c0), (c1, -s1), (-s1, -c1)]
        for i, (a, b) in enumerate(rows):
            full[group, i * PER_RES:(i + 1) * PER_RES, 0] = a
            full[group, i * PER_RES:(i + 1) * PER_RES, 1] = b
    full = full.reshape(4, 4 * PER_RES, 2 * FOLDED).astype(np.float32)
    high = full.astype(BF16)
    low = (full - high.astype(np.float32)).astype(BF16)
    return high, low


def lag_table():
    shifts = np.arange(LAGS) - LAGS // 2
    angle = 2.0 * np.pi / SAMPLES * (((BAND_START + BIN_ORDER)[None, :] * shifts[:, None]) % SAMPLES)
    return np.concatenate([np.cos(angle), -np.sin(angle)], axis=1).astype(np.float32).astype(BF16)


def window_table():
    return (np.abs(BIN_ORDER[:, None] - BIN_ORDER[None, :]) <= HALF).astype(BF16)


def split(value):
    high = value.astype(jnp.bfloat16)
    return high, (value - high.astype(jnp.float32)).astype(jnp.bfloat16)


def dot_nt(a, b):
    return lax.dot_general(a, b, (((1,), (1,)), ((), ())), preferred_element_type=jnp.float32)


def dot_nn(a, b):
    return jnp.dot(a, b, preferred_element_type=jnp.float32)


def list_pairs(offsets_ref, counts_ref, owner_ref, index_ref):
    blocks = counts_ref.shape[0]
    my_start = lax.axis_index("chan") * TILE_DEV
    for i in range(2 * TILE_DEV):
        index_ref[i] = 0
    index_ref[2 * TILE_DEV] = lax.axis_index("seg")

    def one_block(a, start):
        def one_pair(rank, carry):
            slot = owner_ref[start + rank] - my_start

            @pl.when((slot >= 0) & (slot < TILE_DEV))
            def _():
                index_ref[slot] = a
                index_ref[TILE_DEV + slot] = lax.rem(a + offsets_ref[a, rank], blocks)

            return carry

        lax.fori_loop(0, counts_ref[a], one_pair, 0)
        return start + counts_ref[a]

    lax.fori_loop(0, blocks, one_block, 0)


def whiten_kernel(x_ref, high_ref, low_ref, near_ref, offsets_ref, counts_ref, owner_ref,
                  out_ref, index_ref, folded, total):
    step = pl.program_id(0)
    block_size = x_ref.shape[0]
    segs = out_ref.shape[0]
    deep = PARTS * segs
    some = 2

    @pl.when(step == 0)
    def _():
        list_pairs(offsets_ref, counts_ref, owner_ref, index_ref)

        def fold(i, carry):
            at = i * some
            x = [
                x_ref[pl.ds(at, some), j * deep:(j + 1) * deep, :].astype(jnp.float32)
                for j in range(RADIX)
            ]
            e0, e1, e2, e3 = x[0] + x[4], x[1] + x[5], x[2] + x[6], x[3] + x[7]
            d0, d1, d2, d3 = x[0] - x[4], x[1] - x[5], x[2] - x[6], x[3] - x[7]
            root = math.sqrt(0.5)
            plus, minus = (d1 + d3) * root, (d1 - d3) * root
            values = (
                (e0 + e2) + (e1 + e3), (e0 + e2) - (e1 + e3),
                d0 + minus, -(d2 + plus),
                e0 - e2, e3 - e1,
                d0 - minus, d2 - plus,
            )
            for j, value in enumerate(values):
                rows = pl.ds(pl.multiple_of(at * deep, some * deep), some * deep)
                folded[j // 2, j % 2, rows, :] = value.reshape(some * deep, LANES)
            return carry

        lax.fori_loop(0, block_size // some, fold, 0, unroll=2)

    pieces = []
    for half in range(2):
        for part in range(PARTS):
            column = [
                folded[step, half, pl.ds(part * segs + s, block_size, stride=deep), :]
                for s in range(segs)
            ]
            pieces.append(split(jnp.concatenate(column, axis=0)))
    y_high = jnp.concatenate([piece[0] for piece in pieces], axis=1)
    y_low = jnp.concatenate([piece[1] for piece in pieces], axis=1)
    t_high = high_ref[0]
    total[step] = dot_nt(t_high, y_high) + dot_nt(t_high, y_low) + dot_nt(low_ref[0], y_high)

    @pl.when(step == pl.num_programs(0) - 1)
    def _():
        real, imag, counts = [], [], []
        width = segs * block_size
        for group in range(4):
            for half in range(2):
                base = half * 2 * PER_RES
                real.append(total[group, base:base + PER_RES])
                imag.append(total[group, base + PER_RES:base + 2 * PER_RES])
                bins = lax.broadcasted_iota(jnp.int32, (PER_RES, width), 0) * RADIX
                bins = bins + RESIDUES[2 * group + half]
                ends = jnp.minimum(bins + HALF, FREQS - 1) - jnp.maximum(bins - HALF, 0)
                counts.append((ends + 1).astype(jnp.float32))
        real = jnp.concatenate(real, axis=0)
        imag = jnp.concatenate(imag, axis=0)
        amplitude = jnp.sqrt(real * real + imag * imag)
        high = amplitude.astype(jnp.bfloat16)
        mid, low = split(amplitude - high.astype(jnp.float32))
        near = near_ref[...]
        summed = dot_nn(near, high) + (dot_nn(near, mid) + dot_nn(near, low))
        divisor = jnp.maximum(summed / jnp.concatenate(counts, axis=0), 1.0)
        for part, value in enumerate((real, imag)):
            white = (value / divisor).astype(jnp.bfloat16)
            for s in range(segs):
                out_ref[s, part] = white[:, s * block_size:(s + 1) * block_size]


def whiten(traces, pair_offsets, pair_counts, pair_owner):
    block_size, segs, samples = traces.shape
    pieces = samples // LANES
    laid = traces.reshape(block_size, segs, pieces, LANES).transpose(0, 2, 1, 3)
    laid = laid.reshape(block_size, pieces * segs, LANES)
    high, low = dft_tables()
    once = lambda shape: pl.BlockSpec(shape, lambda g: (0,) * len(shape))
    table = pl.BlockSpec((1, 4 * PER_RES, 2 * FOLDED), lambda g: (g, 0, 0))
    scalars = pl.BlockSpec(memory_space=pltpu.SMEM)
    return pl.pallas_call(
        whiten_kernel,
        grid=(4,),
        in_specs=[once(laid.shape), table, table, once((FREQS, FREQS)), scalars, scalars, scalars],
        out_specs=[once((segs, 2, FREQS, block_size)), scalars],
        out_shape=[
            jax.ShapeDtypeStruct((segs, 2, FREQS, block_size), jnp.bfloat16),
            jax.ShapeDtypeStruct((8,), jnp.int32),
        ],
        scratch_shapes=[
            pltpu.VMEM((4, 2, block_size * PARTS * segs, LANES), jnp.float32),
            pltpu.VMEM((4, 4 * PER_RES, block_size * segs), jnp.float32),
        ],
        compiler_params=pltpu.CompilerParams(vmem_limit_bytes=56 << 20),
    )(laid, jnp.asarray(high), jnp.asarray(low), jnp.asarray(window_table()),
      pair_offsets, pair_counts, pair_owner)


PLANES = 4
MESH = pl.DeviceIdType.MESH
LINE_ROWS = 1792


def gather_kernel(own_ref, all_ref, z_send, z_recv, p_send, p_recv, c_send, c_recv,
                  bz_send, bz_recv, bp_send, bp_recv, bc_send, bc_recv, own_sem):
    chan, seg = lax.axis_index("chan"), lax.axis_index("seg")
    y, x, core = chan // 4, (chan // 2) % 2, chan % 2
    x_near = 4 * y + 2 * (1 - x) + core
    y_near = 4 * (1 - y) + 2 * x + core
    across = 4 * (1 - y) + 2 * (1 - x) + core
    twin = 4 * y + 2 * x + (1 - core)
    blocks = (chan, x_near, y_near, across)
    twin_blocks = [block + 1 - 2 * core for block in blocks]
    near = (x_near, y_near)
    total_rows = own_ref.shape[0]
    line = pl.ds(0, LINE_ROWS)
    line_half = [pl.ds(h * (LINE_ROWS // 2), LINE_ROWS // 2) for h in (0, 1)]
    rest_rows = total_rows - LINE_ROWS
    rest = pl.ds(LINE_ROWS, rest_rows)
    rest_half = [pl.ds(LINE_ROWS + h * (rest_rows // 2), rest_rows // 2) for h in (0, 1)]

    barrier = pltpu.get_barrier_semaphore()
    for other in (x_near, y_near, twin):
        pl.semaphore_signal(barrier, inc=1, device_id=(other, seg), device_id_type=MESH)

    def program(z):
        for step in (1, -1):
            if 0 <= z + step < PLANES:
                pl.semaphore_signal(barrier, inc=1, device_id=(chan, z + step), device_id_type=MESH)
        pl.semaphore_wait(barrier, 3 + int(z > 0) + int(z < PLANES - 1))
        sent = []
        order = sorted(range(PLANES), key=lambda other: abs(other - z))

        def send(src, dst, send_sem, recv_sem, device):
            copy = pltpu.make_async_remote_copy(
                src_ref=src, dst_ref=dst, send_sem=send_sem, recv_sem=recv_sem,
                device_id=device, device_id_type=MESH,
            )
            copy.start()
            sent.append(copy)

        def landed(ref, sem):
            pltpu.make_async_remote_copy(
                src_ref=ref, dst_ref=ref, send_sem=sem, recv_sem=sem,
                device_id=(twin, z), device_id_type=MESH,
            ).wait_recv()

        def part(block, other, rows):
            if block == 0 and other == z:
                return own_ref.at[rows]
            return all_ref.at[blocks[block], other, rows]

        def along(block, other, rows, send_sem, recv_sem):
            for step, side in ((1, 0), (-1, 1)):
                away = other == z or (z - other) * step > 0
                if away and 0 <= z + step < PLANES:
                    send(part(block, other, rows), all_ref.at[blocks[block], other, rows],
                         send_sem.at[other, block, side], recv_sem.at[other, block], (chan, z + step))

        def to_twin(block, other, rows, send_sem, recv_sem, half):
            send(part(block, other, rows), all_ref.at[blocks[block], other, rows],
                 send_sem.at[other, block, half], recv_sem.at[other, block, half], (twin, z))

        def outward(other, halves, send_sem, recv_sem):
            for first in (0, 1):
                for way in (0, 1):
                    half = first if way == 0 else 1 - first
                    send(part(0, other, halves[half]), all_ref.at[chan, other, halves[half]],
                         send_sem.at[other, way, half], recv_sem.at[other, way, half], (near[way], z))

        def onward(other, halves, send_sem, recv_sem, first):
            for way in (0, 1):
                half = first if way == 0 else 1 - first
                ref = all_ref.at[near[way], other, halves[half]]
                landed(ref, recv_sem.at[other, way, half])
                if half == way:
                    send(ref, ref, send_sem.at[other, 2, half], recv_sem.at[other, 2, half],
                         (near[1 - way], z))

        def finish(other, halves, recv_sem):
            for half in (0, 1):
                landed(all_ref.at[across, other, halves[half]], recv_sem.at[other, 2, half])

        def line_out(other):
            outward(other, line_half, p_send, p_recv)
            for half in (0, 1):
                to_twin(0, other, line_half[half], c_send, c_recv, half)

        def line_on(other):
            for first in (0, 1):
                onward(other, line_half, p_send, p_recv, first)
                to_twin(1, other, line_half[first], c_send, c_recv, first)
                to_twin(2, other, line_half[1 - first], c_send, c_recv, 1 - first)

        def line_finish(other):
            finish(other, line_half, p_recv)
            for half in (0, 1):
                to_twin(3, other, line_half[half], c_send, c_recv, half)

        def rest_line(other):
            for block in range(4):
                landed(all_ref.at[blocks[block], other, rest], bz_recv.at[other, block])
                along(block, other, rest, bz_send, bz_recv)
                to_twin(block, other, rest, bc_send, bc_recv, 0)

        along(0, z, line, z_send, z_recv)
        outward(z, rest_half, bp_send, bp_recv)
        along(0, z, rest, bz_send, bz_recv)
        to_twin(0, z, rest, bc_send, bc_recv, 0)
        local = pltpu.make_async_copy(own_ref, all_ref.at[chan, z], own_sem)
        local.start()
        line_out(z)
        for first in (0, 1):
            onward(z, rest_half, bp_send, bp_recv, first)
        for block in (1, 2):
            along(block, z, rest, bz_send, bz_recv)
            to_twin(block, z, rest, bc_send, bc_recv, 0)
        finish(z, rest_half, bp_recv)
        along(3, z, rest, bz_send, bz_recv)
        to_twin(3, z, rest, bc_send, bc_recv, 0)
        for k in range(1, PLANES):
            landed(all_ref.at[chan, order[k], line], z_recv.at[order[k], 0])
            along(0, order[k], line, z_send, z_recv)
            line_out(order[k])
            line_on(order[k - 1])
            rest_line(order[k])
            if k > 1:
                line_finish(order[k - 2])
        line_on(order[-1])
        line_finish(order[-2])
        line_finish(order[-1])
        for other in range(PLANES):
            for block in range(4):
                ref = all_ref.at[twin_blocks[block], other]
                for half in (0, 1):
                    landed(ref.at[line_half[half]], c_recv.at[other, block, half])
                landed(ref.at[rest], bc_recv.at[other, block, 0])
        for copy in sent:
            copy.wait_send()
        local.wait()

    for z in range(PLANES):
        pl.when(seg == z)(functools.partial(program, z))


def gather(own):
    dma = pltpu.SemaphoreType.DMA
    rows, lanes = math.prod(own.shape[:-1]), own.shape[-1]
    gathered = pl.pallas_call(
        gather_kernel,
        in_specs=[pl.BlockSpec(memory_space=pl.ANY)],
        out_specs=pl.BlockSpec(memory_space=pl.ANY),
        out_shape=jax.ShapeDtypeStruct((8, PLANES, rows, lanes), own.dtype),
        scratch_shapes=[
            dma((PLANES, 1, 2)), dma((PLANES, 1)),
            dma((PLANES, 3, 2)), dma((PLANES, 3, 2)),
            dma((PLANES, 4, 2)), dma((PLANES, 4, 2)),
            dma((PLANES, 4, 2)), dma((PLANES, 4)),
            dma((PLANES, 3, 2)), dma((PLANES, 3, 2)),
            dma((PLANES, 4, 1)), dma((PLANES, 4, 1)), dma,
        ],
        compiler_params=pltpu.CompilerParams(collective_id=0, has_side_effects=True),
    )(own.reshape(rows, lanes))
    return gathered.reshape((8, PLANES) + own.shape)


GROUP = 16
FCHUNK = 128
CROSS_STEPS = FREQS // FCHUNK
ROWS_STEP = 8


def stack_kernel(norm_factor, parts, segs, rows, index_ref, first_ref, second_ref, table_ref, out_ref, cross):
    step = pl.program_id(1)
    depth = parts * segs * 2 * GROUP
    block = second_ref.shape[-1]

    @pl.when(step < CROSS_STEPS)
    def _():
        own = index_ref[4] * rows
        select = (
            lax.broadcasted_iota(jnp.int32, (rows, block), 1)
            == lax.broadcasted_iota(jnp.int32, (rows, block), 0) + own
        ).astype(jnp.bfloat16)
        mask = (
            lax.broadcasted_iota(jnp.int32, (rows, GROUP, depth), 2) % GROUP
            == lax.broadcasted_iota(jnp.int32, (rows, GROUP, depth), 1)
        )
        for g in range(FCHUNK // GROUP):
            span = slice(g * GROUP, (g + 1) * GROUP)
            firsts, plain, turned = [], [], []
            for z in range(parts):
                for s in range(segs):
                    firsts += [first_ref[0, z, s, p, span] for p in range(2)]
                    re, im = second_ref[0, z, s, 0, span], second_ref[0, z, s, 1, span]
                    plain += [re, im]
                    turned += [-im, re]
            left = dot_nt(select, jnp.concatenate(firsts, axis=0))
            wide = jnp.broadcast_to(left[:, None, :], (rows, GROUP, depth))
            wide = jnp.where(mask, wide, 0.0).reshape(rows * GROUP, depth).astype(jnp.bfloat16)
            right = jnp.concatenate(
                [jnp.concatenate(plain, axis=0), jnp.concatenate(turned, axis=0)], axis=1
            )
            result = dot_nn(wide, right).astype(jnp.bfloat16).reshape(rows, GROUP, 2 * block)
            at = pl.multiple_of(step * FCHUNK + g * GROUP, GROUP)
            cross[:, 0, pl.ds(at, GROUP), :] = result[:, :, :block]
            cross[:, 1, pl.ds(at, GROUP), :] = result[:, :, block:]

    @pl.when(step >= CROSS_STEPS)
    def _():
        base = (step - CROSS_STEPS) * ROWS_STEP
        table = table_ref[...]
        for pair in range(ROWS_STEP // 2):
            both = [
                cross[base + 2 * pair + h].reshape(2 * FREQS, block) for h in range(2)
            ]
            lagged = dot_nn(table, jnp.concatenate(both, axis=1)) * norm_factor
            for h in range(2):
                out_ref[2 * pair + h, 0] = lagged[:, h * block:(h + 1) * block].T


def stack(index, gathered, norm_factor, rows):
    _, parts, segs, _, _, block = gathered.shape
    grid = (TILE_DEV, CROSS_STEPS + rows // ROWS_STEP)
    shape = (1, parts, segs, 2, FCHUNK, block)

    def place(offset, slot, step, index_ref):
        return (index_ref[offset + slot], 0, 0, 0, jnp.minimum(step, CROSS_STEPS - 1), 0)

    return pl.pallas_call(
        functools.partial(stack_kernel, norm_factor, parts, segs, rows),
        grid_spec=pltpu.PrefetchScalarGridSpec(
            num_scalar_prefetch=1,
            grid=grid,
            in_specs=[
                pl.BlockSpec(shape, functools.partial(place, 0)),
                pl.BlockSpec(shape, functools.partial(place, TILE_DEV)),
                pl.BlockSpec((LAGS, 2 * FREQS), lambda slot, step, index_ref: (0, 0)),
            ],
            out_specs=pl.BlockSpec(
                (ROWS_STEP, 1, block, LAGS),
                lambda slot, step, index_ref: (jnp.maximum(step - CROSS_STEPS, 0), slot, 0, 0),
            ),
            scratch_shapes=[pltpu.VMEM((rows, 2, FREQS, block), jnp.bfloat16)],
        ),
        out_shape=jax.ShapeDtypeStruct((rows, TILE_DEV, block, LAGS), jnp.float32),
        compiler_params=pltpu.CompilerParams(vmem_limit_bytes=48 << 20),
    )(index, gathered, gathered, jnp.asarray(lag_table()))


def on_device(traces, pair_offsets, pair_counts, pair_owner):
    block_size, local_segs, sample_count = traces.shape
    parts_count = lax.axis_size("seg")
    block_count = lax.axis_size("chan")
    norm_factor = 1.0 / math.sqrt(FREQS * local_segs * parts_count)
    whitened, index = whiten(traces, pair_offsets, pair_counts, pair_owner)
    if (block_count, parts_count) == (8, PLANES):
        gathered = gather(whitened)
    else:
        gathered = lax.all_gather(lax.all_gather(whitened, "seg", axis=0), "chan", axis=0)
    return stack(index, gathered, norm_factor, block_size // parts_count)


def solution(mesh):
    placed = (P("chan", "seg", None), P(), P(), P())
    return jax.shard_map(
        on_device,
        mesh=mesh,
        in_specs=placed,
        out_specs=P("seg", "chan", None, None),
        check_vma=False,
    )
```

```python
import functools
import math

import jax
import jax.numpy as jnp
import ml_dtypes
import numpy as np
from jax import lax
from jax.experimental import pallas as pl
from jax.experimental.pallas import tpu as pltpu
from jax.sharding import PartitionSpec as P

SAMPLES = 8192
BAND_START = 32
FREQS = 512
HALF = 8
LAGS = 256
TILE_DEV = 2

RADIX = 8
FOLDED = SAMPLES // RADIX
RESIDUES = (0, 4, 1, 7, 2, 6, 3, 5)
PER_RES = FREQS // RADIX
LANES = 128
PARTS = FOLDED // LANES
BF16 = ml_dtypes.bfloat16

BIN_ORDER = np.concatenate([np.arange(PER_RES) * RADIX + r for r in RESIDUES])


def dft_tables():
    n = np.arange(FOLDED)
    full = np.zeros((4, 4 * PER_RES, 2, FOLDED))
    for group in range(4):
        first, second = RESIDUES[2 * group], RESIDUES[2 * group + 1]
        parts = []
        for r in (first, second):
            k = BAND_START + np.arange(PER_RES) * RADIX + r
            angle = 2.0 * np.pi / SAMPLES * ((k[:, None] * n[None, :]) % SAMPLES)
            parts.append((np.cos(angle), np.sin(angle)))
        (c0, s0), (c1, s1) = parts
        o = np.zeros_like(c0)
        if group == 0:
            rows = [(c0, o), (-s0, o), (o, c1), (o, -s1)]
        else:
            rows = [(c0, s0), (-s0, c0), (c1, -s1), (-s1, -c1)]
        for i, (a, b) in enumerate(rows):
            full[group, i * PER_RES:(i + 1) * PER_RES, 0] = a
            full[group, i * PER_RES:(i + 1) * PER_RES, 1] = b
    full = full.reshape(4, 4 * PER_RES, 2 * FOLDED).astype(np.float32)
    high = full.astype(BF16)
    low = (full - high.astype(np.float32)).astype(BF16)
    return high, low


def lag_table():
    shifts = np.arange(LAGS) - LAGS // 2
    angle = 2.0 * np.pi / SAMPLES * (((BAND_START + BIN_ORDER)[None, :] * shifts[:, None]) % SAMPLES)
    return np.concatenate([np.cos(angle), -np.sin(angle)], axis=1).astype(np.float32).astype(BF16)


def window_table():
    return (np.abs(BIN_ORDER[:, None] - BIN_ORDER[None, :]) <= HALF).astype(BF16)


def split(value):
    high = value.astype(jnp.bfloat16)
    return high, (value - high.astype(jnp.float32)).astype(jnp.bfloat16)


def dot_nt(a, b):
    return lax.dot_general(a, b, (((1,), (1,)), ((), ())), preferred_element_type=jnp.float32)


def dot_nn(a, b):
    return jnp.dot(a, b, preferred_element_type=jnp.float32)


def list_pairs(offsets_ref, counts_ref, owner_ref, index_ref):
    blocks = counts_ref.shape[0]
    my_start = lax.axis_index("chan") * TILE_DEV
    for i in range(2 * TILE_DEV):
        index_ref[i] = 0
    index_ref[2 * TILE_DEV] = lax.axis_index("seg")

    def one_block(a, start):
        def one_pair(rank, carry):
            slot = owner_ref[start + rank] - my_start

            @pl.when((slot >= 0) & (slot < TILE_DEV))
            def _():
                index_ref[slot] = a
                index_ref[TILE_DEV + slot] = lax.rem(a + offsets_ref[a, rank], blocks)

            return carry

        lax.fori_loop(0, counts_ref[a], one_pair, 0)
        return start + counts_ref[a]

    lax.fori_loop(0, blocks, one_block, 0)


def whiten_kernel(x_ref, high_ref, low_ref, near_ref, offsets_ref, counts_ref, owner_ref,
                  out_ref, index_ref, folded, total):
    step = pl.program_id(0)
    block_size = x_ref.shape[0]
    segs = out_ref.shape[0]
    deep = PARTS * segs
    some = 2

    @pl.when(step == 0)
    def _():
        list_pairs(offsets_ref, counts_ref, owner_ref, index_ref)

        def fold(i, carry):
            at = i * some
            x = [
                x_ref[pl.ds(at, some), j * deep:(j + 1) * deep, :].astype(jnp.float32)
                for j in range(RADIX)
            ]
            e0, e1, e2, e3 = x[0] + x[4], x[1] + x[5], x[2] + x[6], x[3] + x[7]
            d0, d1, d2, d3 = x[0] - x[4], x[1] - x[5], x[2] - x[6], x[3] - x[7]
            root = math.sqrt(0.5)
            plus, minus = (d1 + d3) * root, (d1 - d3) * root
            values = (
                (e0 + e2) + (e1 + e3), (e0 + e2) - (e1 + e3),
                d0 + minus, -(d2 + plus),
                e0 - e2, e3 - e1,
                d0 - minus, d2 - plus,
            )
            for j, value in enumerate(values):
                rows = pl.ds(pl.multiple_of(at * deep, some * deep), some * deep)
                folded[j // 2, j % 2, rows, :] = value.reshape(some * deep, LANES)
            return carry

        lax.fori_loop(0, block_size // some, fold, 0, unroll=2)

    pieces = []
    for half in range(2):
        for part in range(PARTS):
            column = [
                folded[step, half, pl.ds(part * segs + s, block_size, stride=deep), :]
                for s in range(segs)
            ]
            pieces.append(split(jnp.concatenate(column, axis=0)))
    y_high = jnp.concatenate([piece[0] for piece in pieces], axis=1)
    y_low = jnp.concatenate([piece[1] for piece in pieces], axis=1)
    t_high = high_ref[0]
    total[step] = dot_nt(t_high, y_high) + dot_nt(t_high, y_low) + dot_nt(low_ref[0], y_high)

    @pl.when(step == pl.num_programs(0) - 1)
    def _():
        real, imag, counts = [], [], []
        width = segs * block_size
        for group in range(4):
            for half in range(2):
                base = half * 2 * PER_RES
                real.append(total[group, base:base + PER_RES])
                imag.append(total[group, base + PER_RES:base + 2 * PER_RES])
                bins = lax.broadcasted_iota(jnp.int32, (PER_RES, width), 0) * RADIX
                bins = bins + RESIDUES[2 * group + half]
                ends = jnp.minimum(bins + HALF, FREQS - 1) - jnp.maximum(bins - HALF, 0)
                counts.append((ends + 1).astype(jnp.float32))
        real = jnp.concatenate(real, axis=0)
        imag = jnp.concatenate(imag, axis=0)
        amplitude = jnp.sqrt(real * real + imag * imag)
        high = amplitude.astype(jnp.bfloat16)
        mid, low = split(amplitude - high.astype(jnp.float32))
        near = near_ref[...]
        summed = dot_nn(near, high) + (dot_nn(near, mid) + dot_nn(near, low))
        divisor = jnp.maximum(summed / jnp.concatenate(counts, axis=0), 1.0)
        for part, value in enumerate((real, imag)):
            white = (value / divisor).astype(jnp.bfloat16)
            for s in range(segs):
                out_ref[s, part] = white[:, s * block_size:(s + 1) * block_size]


def whiten(traces, pair_offsets, pair_counts, pair_owner):
    block_size, segs, samples = traces.shape
    pieces = samples // LANES
    laid = traces.reshape(block_size, segs, pieces, LANES).transpose(0, 2, 1, 3)
    laid = laid.reshape(block_size, pieces * segs, LANES)
    high, low = dft_tables()
    once = lambda shape: pl.BlockSpec(shape, lambda g: (0,) * len(shape))
    table = pl.BlockSpec((1, 4 * PER_RES, 2 * FOLDED), lambda g: (g, 0, 0))
    scalars = pl.BlockSpec(memory_space=pltpu.SMEM)
    return pl.pallas_call(
        whiten_kernel,
        grid=(4,),
        in_specs=[once(laid.shape), table, table, once((FREQS, FREQS)), scalars, scalars, scalars],
        out_specs=[once((segs, 2, FREQS, block_size)), scalars],
        out_shape=[
            jax.ShapeDtypeStruct((segs, 2, FREQS, block_size), jnp.bfloat16),
            jax.ShapeDtypeStruct((8,), jnp.int32),
        ],
        scratch_shapes=[
            pltpu.VMEM((4, 2, block_size * PARTS * segs, LANES), jnp.float32),
            pltpu.VMEM((4, 4 * PER_RES, block_size * segs), jnp.float32),
        ],
        compiler_params=pltpu.CompilerParams(vmem_limit_bytes=56 << 20),
    )(laid, jnp.asarray(high), jnp.asarray(low), jnp.asarray(window_table()),
      pair_offsets, pair_counts, pair_owner)


PLANES = 4
MESH = pl.DeviceIdType.MESH
LINE_ROWS = 1664


def gather_kernel(own_ref, all_ref, z_send, z_recv, p_send, p_recv, c_send, c_recv,
                  bz_send, bz_recv, bp_send, bp_recv, bc_send, bc_recv, own_sem):
    chan, seg = lax.axis_index("chan"), lax.axis_index("seg")
    y, x, core = chan // 4, (chan // 2) % 2, chan % 2
    x_near = 4 * y + 2 * (1 - x) + core
    y_near = 4 * (1 - y) + 2 * x + core
    across = 4 * (1 - y) + 2 * (1 - x) + core
    twin = 4 * y + 2 * x + (1 - core)
    blocks = (chan, x_near, y_near, across)
    twin_blocks = [block + 1 - 2 * core for block in blocks]
    near = (x_near, y_near)
    total_rows = own_ref.shape[0]
    line = pl.ds(0, LINE_ROWS)
    line_half = [pl.ds(h * (LINE_ROWS // 2), LINE_ROWS // 2) for h in (0, 1)]
    rest_rows = total_rows - LINE_ROWS
    rest = pl.ds(LINE_ROWS, rest_rows)
    rest_half = [pl.ds(LINE_ROWS + h * (rest_rows // 2), rest_rows // 2) for h in (0, 1)]

    barrier = pltpu.get_barrier_semaphore()
    for other in (x_near, y_near, twin):
        pl.semaphore_signal(barrier, inc=1, device_id=(other, seg), device_id_type=MESH)

    def program(z):
        for step in (1, -1):
            if 0 <= z + step < PLANES:
                pl.semaphore_signal(barrier, inc=1, device_id=(chan, z + step), device_id_type=MESH)
        pl.semaphore_wait(barrier, 3 + int(z > 0) + int(z < PLANES - 1))
        sent = []
        order = sorted(range(PLANES), key=lambda other: abs(other - z))

        def send(src, dst, send_sem, recv_sem, device):
            copy = pltpu.make_async_remote_copy(
                src_ref=src, dst_ref=dst, send_sem=send_sem, recv_sem=recv_sem,
                device_id=device, device_id_type=MESH,
            )
            copy.start()
            sent.append(copy)

        def landed(ref, sem):
            pltpu.make_async_remote_copy(
                src_ref=ref, dst_ref=ref, send_sem=sem, recv_sem=sem,
                device_id=(twin, z), device_id_type=MESH,
            ).wait_recv()

        def part(block, other, rows):
            if block == 0 and other == z:
                return own_ref.at[rows]
            return all_ref.at[blocks[block], other, rows]

        def along(block, other, rows, send_sem, recv_sem):
            for step, side in ((1, 0), (-1, 1)):
                away = other == z or (z - other) * step > 0
                if away and 0 <= z + step < PLANES:
                    send(part(block, other, rows), all_ref.at[blocks[block], other, rows],
                         send_sem.at[other, block, side], recv_sem.at[other, block], (chan, z + step))

        def to_twin(block, other, rows, send_sem, recv_sem, half):
            send(part(block, other, rows), all_ref.at[blocks[block], other, rows],
                 send_sem.at[other, block, half], recv_sem.at[other, block, half], (twin, z))

        def outward(other, halves, send_sem, recv_sem):
            for first in (0, 1):
                for way in (0, 1):
                    half = first if way == 0 else 1 - first
                    send(part(0, other, halves[half]), all_ref.at[chan, other, halves[half]],
                         send_sem.at[other, way, half], recv_sem.at[other, way, half], (near[way], z))

        def onward(other, halves, send_sem, recv_sem, first):
            for way in (0, 1):
                half = first if way == 0 else 1 - first
                ref = all_ref.at[near[way], other, halves[half]]
                landed(ref, recv_sem.at[other, way, half])
                if half == way:
                    send(ref, ref, send_sem.at[other, 2, half], recv_sem.at[other, 2, half],
                         (near[1 - way], z))

        def finish(other, halves, recv_sem):
            for half in (0, 1):
                landed(all_ref.at[across, other, halves[half]], recv_sem.at[other, 2, half])

        def line_out(other):
            outward(other, line_half, p_send, p_recv)
            for half in (0, 1):
                to_twin(0, other, line_half[half], c_send, c_recv, half)

        def line_on(other):
            for first in (0, 1):
                onward(other, line_half, p_send, p_recv, first)
                to_twin(1, other, line_half[first], c_send, c_recv, first)
                to_twin(2, other, line_half[1 - first], c_send, c_recv, 1 - first)

        def line_finish(other):
            finish(other, line_half, p_recv)
            for half in (0, 1):
                to_twin(3, other, line_half[half], c_send, c_recv, half)

        def rest_line(other):
            for block in range(4):
                landed(all_ref.at[blocks[block], other, rest], bz_recv.at[other, block])
                along(block, other, rest, bz_send, bz_recv)
                to_twin(block, other, rest, bc_send, bc_recv, 0)

        along(0, z, line, z_send, z_recv)
        outward(z, rest_half, bp_send, bp_recv)
        along(0, z, rest, bz_send, bz_recv)
        to_twin(0, z, rest, bc_send, bc_recv, 0)
        local = pltpu.make_async_copy(own_ref, all_ref.at[chan, z], own_sem)
        local.start()
        line_out(z)
        for first in (0, 1):
            onward(z, rest_half, bp_send, bp_recv, first)
        for block in (1, 2):
            along(block, z, rest, bz_send, bz_recv)
            to_twin(block, z, rest, bc_send, bc_recv, 0)
        finish(z, rest_half, bp_recv)
        along(3, z, rest, bz_send, bz_recv)
        to_twin(3, z, rest, bc_send, bc_recv, 0)
        for k in range(1, PLANES):
            landed(all_ref.at[chan, order[k], line], z_recv.at[order[k], 0])
            along(0, order[k], line, z_send, z_recv)
            line_out(order[k])
            line_on(order[k - 1])
            rest_line(order[k])
            if k > 1:
                line_finish(order[k - 2])
        line_on(order[-1])
        line_finish(order[-2])
        line_finish(order[-1])
        for other in range(PLANES):
            for block in range(4):
                ref = all_ref.at[twin_blocks[block], other]
                for half in (0, 1):
                    landed(ref.at[line_half[half]], c_recv.at[other, block, half])
                landed(ref.at[rest], bc_recv.at[other, block, 0])
        for copy in sent:
            copy.wait_send()
        local.wait()

    for z in range(PLANES):
        pl.when(seg == z)(functools.partial(program, z))


def gather(own):
    dma = pltpu.SemaphoreType.DMA
    rows, lanes = math.prod(own.shape[:-1]), own.shape[-1]
    gathered = pl.pallas_call(
        gather_kernel,
        in_specs=[pl.BlockSpec(memory_space=pl.ANY)],
        out_specs=pl.BlockSpec(memory_space=pl.ANY),
        out_shape=jax.ShapeDtypeStruct((8, PLANES, rows, lanes), own.dtype),
        scratch_shapes=[
            dma((PLANES, 1, 2)), dma((PLANES, 1)),
            dma((PLANES, 3, 2)), dma((PLANES, 3, 2)),
            dma((PLANES, 4, 2)), dma((PLANES, 4, 2)),
            dma((PLANES, 4, 2)), dma((PLANES, 4)),
            dma((PLANES, 3, 2)), dma((PLANES, 3, 2)),
            dma((PLANES, 4, 1)), dma((PLANES, 4, 1)), dma,
        ],
        compiler_params=pltpu.CompilerParams(collective_id=0, has_side_effects=True),
    )(own.reshape(rows, lanes))
    return gathered.reshape((8, PLANES) + own.shape)


GROUP = 16
FCHUNK = 256
CROSS_STEPS = FREQS // FCHUNK
ROWS_STEP = 16


def stack_kernel(norm_factor, parts, segs, rows, index_ref, first_ref, second_ref, table_ref, out_ref, cross):
    step = pl.program_id(1)
    depth = parts * segs * 2 * GROUP
    block = second_ref.shape[-1]

    @pl.when(step < CROSS_STEPS)
    def _():
        own = index_ref[4] * rows
        select = (
            lax.broadcasted_iota(jnp.int32, (rows, block), 1)
            == lax.broadcasted_iota(jnp.int32, (rows, block), 0) + own
        ).astype(jnp.bfloat16)
        mask = (
            lax.broadcasted_iota(jnp.int32, (rows, GROUP, depth), 2) % GROUP
            == lax.broadcasted_iota(jnp.int32, (rows, GROUP, depth), 1)
        )
        for g in range(FCHUNK // GROUP):
            span = slice(g * GROUP, (g + 1) * GROUP)
            firsts, plain, turned = [], [], []
            for z in range(parts):
                for s in range(segs):
                    firsts += [first_ref[0, z, s, p, span] for p in range(2)]
                    re, im = second_ref[0, z, s, 0, span], second_ref[0, z, s, 1, span]
                    plain += [re, im]
                    turned += [-im, re]
            left = dot_nt(select, jnp.concatenate(firsts, axis=0))
            wide = jnp.broadcast_to(left[:, None, :], (rows, GROUP, depth))
            wide = jnp.where(mask, wide, 0.0).reshape(rows * GROUP, depth).astype(jnp.bfloat16)
            right = jnp.concatenate(
                [jnp.concatenate(plain, axis=0), jnp.concatenate(turned, axis=0)], axis=1
            )
            result = dot_nn(wide, right).astype(jnp.bfloat16).reshape(rows, GROUP, 2 * block)
            at = pl.multiple_of(step * FCHUNK + g * GROUP, GROUP)
            cross[:, 0, pl.ds(at, GROUP), :] = result[:, :, :block]
            cross[:, 1, pl.ds(at, GROUP), :] = result[:, :, block:]

    @pl.when(step >= CROSS_STEPS)
    def _():
        base = (step - CROSS_STEPS) * ROWS_STEP
        table = table_ref[...]
        for pair in range(ROWS_STEP // 2):
            both = [
                cross[base + 2 * pair + h].reshape(2 * FREQS, block) for h in range(2)
            ]
            lagged = dot_nn(table, jnp.concatenate(both, axis=1)) * norm_factor
            for h in range(2):
                out_ref[2 * pair + h, 0] = lagged[:, h * block:(h + 1) * block].T


def stack(index, gathered, norm_factor, rows):
    _, parts, segs, _, _, block = gathered.shape
    grid = (TILE_DEV, CROSS_STEPS + rows // ROWS_STEP)
    shape = (1, parts, segs, 2, FCHUNK, block)

    def place(offset, slot, step, index_ref):
        return (index_ref[offset + slot], 0, 0, 0, jnp.minimum(step, CROSS_STEPS - 1), 0)

    return pl.pallas_call(
        functools.partial(stack_kernel, norm_factor, parts, segs, rows),
        grid_spec=pltpu.PrefetchScalarGridSpec(
            num_scalar_prefetch=1,
            grid=grid,
            in_specs=[
                pl.BlockSpec(shape, functools.partial(place, 0)),
                pl.BlockSpec(shape, functools.partial(place, TILE_DEV)),
                pl.BlockSpec((LAGS, 2 * FREQS), lambda slot, step, index_ref: (0, 0)),
            ],
            out_specs=pl.BlockSpec(
                (ROWS_STEP, 1, block, LAGS),
                lambda slot, step, index_ref: (jnp.maximum(step - CROSS_STEPS, 0), slot, 0, 0),
            ),
            scratch_shapes=[pltpu.VMEM((rows, 2, FREQS, block), jnp.bfloat16)],
        ),
        out_shape=jax.ShapeDtypeStruct((rows, TILE_DEV, block, LAGS), jnp.float32),
        compiler_params=pltpu.CompilerParams(vmem_limit_bytes=48 << 20),
    )(index, gathered, gathered, jnp.asarray(lag_table()))


def on_device(traces, pair_offsets, pair_counts, pair_owner):
    block_size, local_segs, sample_count = traces.shape
    parts_count = lax.axis_size("seg")
    block_count = lax.axis_size("chan")
    norm_factor = 1.0 / math.sqrt(FREQS * local_segs * parts_count)
    whitened, index = whiten(traces, pair_offsets, pair_counts, pair_owner)
    if (block_count, parts_count) == (8, PLANES):
        gathered = gather(whitened)
    else:
        gathered = lax.all_gather(lax.all_gather(whitened, "seg", axis=0), "chan", axis=0)
    return stack(index, gathered, norm_factor, block_size // parts_count)


def solution(mesh):
    placed = (P("chan", "seg", None), P(), P(), P())
    return jax.shard_map(
        on_device,
        mesh=mesh,
        in_specs=placed,
        out_specs=P("seg", "chan", None, None),
        check_vma=False,
    )
```

```python
import functools
import math

import jax
import jax.numpy as jnp
import ml_dtypes
import numpy as np
from jax import lax
from jax.experimental import pallas as pl
from jax.experimental.pallas import tpu as pltpu
from jax.sharding import PartitionSpec as P

SAMPLES = 8192
BAND_START = 32
FREQS = 512
HALF = 8
LAGS = 256
TILE_DEV = 2

RADIX = 8
FOLDED = SAMPLES // RADIX
RESIDUES = (0, 4, 1, 7, 2, 6, 3, 5)
PER_RES = FREQS // RADIX
LANES = 128
PARTS = FOLDED // LANES
BF16 = ml_dtypes.bfloat16

BIN_ORDER = np.concatenate([np.arange(PER_RES) * RADIX + r for r in RESIDUES])


def dft_tables():
    n = np.arange(FOLDED)
    full = np.zeros((4, 4 * PER_RES, 2, FOLDED))
    for group in range(4):
        first, second = RESIDUES[2 * group], RESIDUES[2 * group + 1]
        parts = []
        for r in (first, second):
            k = BAND_START + np.arange(PER_RES) * RADIX + r
            angle = 2.0 * np.pi / SAMPLES * ((k[:, None] * n[None, :]) % SAMPLES)
            parts.append((np.cos(angle), np.sin(angle)))
        (c0, s0), (c1, s1) = parts
        o = np.zeros_like(c0)
        if group == 0:
            rows = [(c0, o), (-s0, o), (o, c1), (o, -s1)]
        else:
            rows = [(c0, s0), (-s0, c0), (c1, -s1), (-s1, -c1)]
        for i, (a, b) in enumerate(rows):
            full[group, i * PER_RES:(i + 1) * PER_RES, 0] = a
            full[group, i * PER_RES:(i + 1) * PER_RES, 1] = b
    full = full.reshape(4, 4 * PER_RES, 2 * FOLDED).astype(np.float32)
    high = full.astype(BF16)
    low = (full - high.astype(np.float32)).astype(BF16)
    return high, low


def lag_table():
    shifts = np.arange(LAGS) - LAGS // 2
    angle = 2.0 * np.pi / SAMPLES * (((BAND_START + BIN_ORDER)[None, :] * shifts[:, None]) % SAMPLES)
    return np.concatenate([np.cos(angle), -np.sin(angle)], axis=1).astype(np.float32).astype(BF16)


def window_table():
    return (np.abs(BIN_ORDER[:, None] - BIN_ORDER[None, :]) <= HALF).astype(BF16)


def split(value):
    high = value.astype(jnp.bfloat16)
    return high, (value - high.astype(jnp.float32)).astype(jnp.bfloat16)


def dot_nt(a, b):
    return lax.dot_general(a, b, (((1,), (1,)), ((), ())), preferred_element_type=jnp.float32)


def dot_nn(a, b):
    return jnp.dot(a, b, preferred_element_type=jnp.float32)


def list_pairs(offsets_ref, counts_ref, owner_ref, index_ref):
    blocks = counts_ref.shape[0]
    my_start = lax.axis_index("chan") * TILE_DEV
    for i in range(2 * TILE_DEV):
        index_ref[i] = 0
    index_ref[2 * TILE_DEV] = lax.axis_index("seg")

    def one_block(a, start):
        def one_pair(rank, carry):
            slot = owner_ref[start + rank] - my_start

            @pl.when((slot >= 0) & (slot < TILE_DEV))
            def _():
                index_ref[slot] = a
                index_ref[TILE_DEV + slot] = lax.rem(a + offsets_ref[a, rank], blocks)

            return carry

        lax.fori_loop(0, counts_ref[a], one_pair, 0)
        return start + counts_ref[a]

    lax.fori_loop(0, blocks, one_block, 0)


def whiten_kernel(x_ref, high_ref, low_ref, near_ref, offsets_ref, counts_ref, owner_ref,
                  out_ref, index_ref, folded, total):
    step = pl.program_id(0)
    block_size = x_ref.shape[0]
    segs = out_ref.shape[0]
    deep = PARTS * segs
    some = 2

    @pl.when(step == 0)
    def _():
        list_pairs(offsets_ref, counts_ref, owner_ref, index_ref)

        def fold(i, carry):
            at = i * some
            x = [
                x_ref[pl.ds(at, some), j * deep:(j + 1) * deep, :].astype(jnp.float32)
                for j in range(RADIX)
            ]
            e0, e1, e2, e3 = x[0] + x[4], x[1] + x[5], x[2] + x[6], x[3] + x[7]
            d0, d1, d2, d3 = x[0] - x[4], x[1] - x[5], x[2] - x[6], x[3] - x[7]
            root = math.sqrt(0.5)
            plus, minus = (d1 + d3) * root, (d1 - d3) * root
            values = (
                (e0 + e2) + (e1 + e3), (e0 + e2) - (e1 + e3),
                d0 + minus, -(d2 + plus),
                e0 - e2, e3 - e1,
                d0 - minus, d2 - plus,
            )
            for j, value in enumerate(values):
                rows = pl.ds(pl.multiple_of(at * deep, some * deep), some * deep)
                folded[j // 2, j % 2, rows, :] = value.reshape(some * deep, LANES)
            return carry

        lax.fori_loop(0, block_size // some, fold, 0, unroll=2)

    pieces = []
    for half in range(2):
        for part in range(PARTS):
            column = [
                folded[step, half, pl.ds(part * segs + s, block_size, stride=deep), :]
                for s in range(segs)
            ]
            pieces.append(split(jnp.concatenate(column, axis=0)))
    y_high = jnp.concatenate([piece[0] for piece in pieces], axis=1)
    y_low = jnp.concatenate([piece[1] for piece in pieces], axis=1)
    t_high = high_ref[0]
    total[step] = dot_nt(t_high, y_high) + dot_nt(t_high, y_low) + dot_nt(low_ref[0], y_high)

    @pl.when(step == pl.num_programs(0) - 1)
    def _():
        real, imag, counts = [], [], []
        width = segs * block_size
        for group in range(4):
            for half in range(2):
                base = half * 2 * PER_RES
                real.append(total[group, base:base + PER_RES])
                imag.append(total[group, base + PER_RES:base + 2 * PER_RES])
                bins = lax.broadcasted_iota(jnp.int32, (PER_RES, width), 0) * RADIX
                bins = bins + RESIDUES[2 * group + half]
                ends = jnp.minimum(bins + HALF, FREQS - 1) - jnp.maximum(bins - HALF, 0)
                counts.append((ends + 1).astype(jnp.float32))
        real = jnp.concatenate(real, axis=0)
        imag = jnp.concatenate(imag, axis=0)
        amplitude = jnp.sqrt(real * real + imag * imag)
        high = amplitude.astype(jnp.bfloat16)
        mid, low = split(amplitude - high.astype(jnp.float32))
        near = near_ref[...]
        summed = dot_nn(near, high) + (dot_nn(near, mid) + dot_nn(near, low))
        divisor = jnp.maximum(summed / jnp.concatenate(counts, axis=0), 1.0)
        for part, value in enumerate((real, imag)):
            white = (value / divisor).astype(jnp.bfloat16)
            for s in range(segs):
                out_ref[s, part] = white[:, s * block_size:(s + 1) * block_size]


def whiten(traces, pair_offsets, pair_counts, pair_owner):
    block_size, segs, samples = traces.shape
    pieces = samples // LANES
    laid = traces.reshape(block_size, segs, pieces, LANES).transpose(0, 2, 1, 3)
    laid = laid.reshape(block_size, pieces * segs, LANES)
    high, low = dft_tables()
    once = lambda shape: pl.BlockSpec(shape, lambda g: (0,) * len(shape))
    table = pl.BlockSpec((1, 4 * PER_RES, 2 * FOLDED), lambda g: (g, 0, 0))
    scalars = pl.BlockSpec(memory_space=pltpu.SMEM)
    return pl.pallas_call(
        whiten_kernel,
        grid=(4,),
        in_specs=[once(laid.shape), table, table, once((FREQS, FREQS)), scalars, scalars, scalars],
        out_specs=[once((segs, 2, FREQS, block_size)), scalars],
        out_shape=[
            jax.ShapeDtypeStruct((segs, 2, FREQS, block_size), jnp.bfloat16),
            jax.ShapeDtypeStruct((8,), jnp.int32),
        ],
        scratch_shapes=[
            pltpu.VMEM((4, 2, block_size * PARTS * segs, LANES), jnp.float32),
            pltpu.VMEM((4, 4 * PER_RES, block_size * segs), jnp.float32),
        ],
        compiler_params=pltpu.CompilerParams(vmem_limit_bytes=56 << 20),
    )(laid, jnp.asarray(high), jnp.asarray(low), jnp.asarray(window_table()),
      pair_offsets, pair_counts, pair_owner)


PLANES = 4
MESH = pl.DeviceIdType.MESH
LINE_ROWS = 1664
Z_AT = 17
ON_AT = 13


def gather_kernel(own_ref, all_ref, z_send, z_recv, p_send, p_recv, c_send, c_recv,
                  bz_send, bz_recv, bp_send, bp_recv, bc_send, bc_recv, own_sem):
    chan, seg = lax.axis_index("chan"), lax.axis_index("seg")
    y, x, core = chan // 4, (chan // 2) % 2, chan % 2
    x_near = 4 * y + 2 * (1 - x) + core
    y_near = 4 * (1 - y) + 2 * x + core
    across = 4 * (1 - y) + 2 * (1 - x) + core
    twin = 4 * y + 2 * x + (1 - core)
    blocks = (chan, x_near, y_near, across)
    twin_blocks = [block + 1 - 2 * core for block in blocks]
    near = (x_near, y_near)
    total_rows = own_ref.shape[0]
    line = pl.ds(0, LINE_ROWS)
    line_half = [pl.ds(h * (LINE_ROWS // 2), LINE_ROWS // 2) for h in (0, 1)]
    rest_rows = total_rows - LINE_ROWS
    rest = pl.ds(LINE_ROWS, rest_rows)
    rest_half = [pl.ds(LINE_ROWS + h * (rest_rows // 2), rest_rows // 2) for h in (0, 1)]

    barrier = pltpu.get_barrier_semaphore()
    for other in (x_near, y_near, twin):
        pl.semaphore_signal(barrier, inc=1, device_id=(other, seg), device_id_type=MESH)

    def program(z):
        for step in (1, -1):
            if 0 <= z + step < PLANES:
                pl.semaphore_signal(barrier, inc=1, device_id=(chan, z + step), device_id_type=MESH)
        pl.semaphore_wait(barrier, 3 + int(z > 0) + int(z < PLANES - 1))
        sent = []
        order = sorted(range(PLANES), key=lambda other: abs(other - z))

        def send(src, dst, send_sem, recv_sem, device):
            copy = pltpu.make_async_remote_copy(
                src_ref=src, dst_ref=dst, send_sem=send_sem, recv_sem=recv_sem,
                device_id=device, device_id_type=MESH,
            )
            copy.start()
            sent.append(copy)

        def landed(ref, sem):
            pltpu.make_async_remote_copy(
                src_ref=ref, dst_ref=ref, send_sem=sem, recv_sem=sem,
                device_id=(twin, z), device_id_type=MESH,
            ).wait_recv()

        def part(block, other, rows):
            if block == 0 and other == z:
                return own_ref.at[rows]
            return all_ref.at[blocks[block], other, rows]

        def along(block, other, rows, send_sem, recv_sem):
            for step, side in ((1, 0), (-1, 1)):
                away = other == z or (z - other) * step > 0
                if away and 0 <= z + step < PLANES:
                    send(part(block, other, rows), all_ref.at[blocks[block], other, rows],
                         send_sem.at[other, block, side], recv_sem.at[other, block], (chan, z + step))

        def to_twin(block, other, rows, send_sem, recv_sem, half):
            send(part(block, other, rows), all_ref.at[blocks[block], other, rows],
                 send_sem.at[other, block, half], recv_sem.at[other, block, half], (twin, z))

        def outward(other, halves, send_sem, recv_sem):
            for first in (0, 1):
                for way in (0, 1):
                    half = first if way == 0 else 1 - first
                    send(part(0, other, halves[half]), all_ref.at[chan, other, halves[half]],
                         send_sem.at[other, way, half], recv_sem.at[other, way, half], (near[way], z))

        def onward(other, halves, send_sem, recv_sem, first):
            for way in (0, 1):
                half = first if way == 0 else 1 - first
                ref = all_ref.at[near[way], other, halves[half]]
                landed(ref, recv_sem.at[other, way, half])
                if half == way:
                    send(ref, ref, send_sem.at[other, 2, half], recv_sem.at[other, 2, half],
                         (near[1 - way], z))

        def finish(other, halves, recv_sem):
            for half in (0, 1):
                landed(all_ref.at[across, other, halves[half]], recv_sem.at[other, 2, half])

        def line_out(other):
            outward(other, line_half, p_send, p_recv)
            for half in (0, 1):
                to_twin(0, other, line_half[half], c_send, c_recv, half)

        def line_on(other):
            for first in (0, 1):
                onward(other, line_half, p_send, p_recv, first)
                to_twin(1, other, line_half[first], c_send, c_recv, first)
                to_twin(2, other, line_half[1 - first], c_send, c_recv, 1 - first)

        def line_finish(other):
            finish(other, line_half, p_recv)
            for half in (0, 1):
                to_twin(3, other, line_half[half], c_send, c_recv, half)

        def line_arrives(other):
            landed(all_ref.at[chan, other, line], z_recv.at[other, 0])
            along(0, other, line, z_send, z_recv)
            line_out(other)

        def rest_line(other):
            for block in range(4):
                landed(all_ref.at[blocks[block], other, rest], bz_recv.at[other, block])
                along(block, other, rest, bz_send, bz_recv)
                to_twin(block, other, rest, bc_send, bc_recv, 0)

        along(0, z, line, z_send, z_recv)
        outward(z, rest_half, bp_send, bp_recv)
        along(0, z, rest, bz_send, bz_recv)
        to_twin(0, z, rest, bc_send, bc_recv, 0)
        local = pltpu.make_async_copy(own_ref, all_ref.at[chan, z], own_sem)
        local.start()
        line_out(z)
        for first in (0, 1):
            onward(z, rest_half, bp_send, bp_recv, first)
        for block in (1, 2):
            along(block, z, rest, bz_send, bz_recv)
            to_twin(block, z, rest, bc_send, bc_recv, 0)
        finish(z, rest_half, bp_recv)
        along(3, z, rest, bz_send, bz_recv)
        to_twin(3, z, rest, bc_send, bc_recv, 0)
        events = [(ON_AT, line_on, z), (ON_AT + 3, line_finish, z)]
        for k in range(1, PLANES):
            far = abs(order[k] - z)
            events += [
                (Z_AT * far - (Z_AT + 1) // 2, line_arrives, order[k]),
                (Z_AT * far, rest_line, order[k]),
                (ON_AT * (k + 1), line_on, order[k]),
                (ON_AT * (k + 1) + 3, line_finish, order[k]),
            ]
        for _, act, other in sorted(events, key=lambda event: event[0]):
            act(other)
        for other in range(PLANES):
            for block in range(4):
                ref = all_ref.at[twin_blocks[block], other]
                for half in (0, 1):
                    landed(ref.at[line_half[half]], c_recv.at[other, block, half])
                landed(ref.at[rest], bc_recv.at[other, block, 0])
        for copy in sent:
            copy.wait_send()
        local.wait()

    for z in range(PLANES):
        pl.when(seg == z)(functools.partial(program, z))


def gather(own):
    dma = pltpu.SemaphoreType.DMA
    rows, lanes = math.prod(own.shape[:-1]), own.shape[-1]
    gathered = pl.pallas_call(
        gather_kernel,
        in_specs=[pl.BlockSpec(memory_space=pl.ANY)],
        out_specs=pl.BlockSpec(memory_space=pl.ANY),
        out_shape=jax.ShapeDtypeStruct((8, PLANES, rows, lanes), own.dtype),
        scratch_shapes=[
            dma((PLANES, 1, 2)), dma((PLANES, 1)),
            dma((PLANES, 3, 2)), dma((PLANES, 3, 2)),
            dma((PLANES, 4, 2)), dma((PLANES, 4, 2)),
            dma((PLANES, 4, 2)), dma((PLANES, 4)),
            dma((PLANES, 3, 2)), dma((PLANES, 3, 2)),
            dma((PLANES, 4, 1)), dma((PLANES, 4, 1)), dma,
        ],
        compiler_params=pltpu.CompilerParams(collective_id=0, has_side_effects=True),
    )(own.reshape(rows, lanes))
    return gathered.reshape((8, PLANES) + own.shape)


GROUP = 16
FCHUNK = 256
CROSS_STEPS = FREQS // FCHUNK
ROWS_STEP = 16


def stack_kernel(norm_factor, parts, segs, rows, index_ref, first_ref, second_ref, table_ref, out_ref, cross):
    step = pl.program_id(1)
    depth = parts * segs * 2 * GROUP
    block = second_ref.shape[-1]

    @pl.when(step < CROSS_STEPS)
    def _():
        own = index_ref[4] * rows
        select = (
            lax.broadcasted_iota(jnp.int32, (rows, block), 1)
            == lax.broadcasted_iota(jnp.int32, (rows, block), 0) + own
        ).astype(jnp.bfloat16)
        mask = (
            lax.broadcasted_iota(jnp.int32, (rows, GROUP, depth), 2) % GROUP
            == lax.broadcasted_iota(jnp.int32, (rows, GROUP, depth), 1)
        ).astype(jnp.bfloat16)
        for g in range(FCHUNK // GROUP):
            span = slice(g * GROUP, (g + 1) * GROUP)
            firsts, plain, turned = [], [], []
            for z in range(parts):
                for s in range(segs):
                    firsts += [first_ref[0, z, s, p, span] for p in range(2)]
                    re, im = second_ref[0, z, s, 0, span], second_ref[0, z, s, 1, span]
                    plain += [re, im]
                    turned += [-im, re]
            left = dot_nt(select, jnp.concatenate(firsts, axis=0))
            wide = jnp.broadcast_to(left.astype(jnp.bfloat16)[:, None, :], (rows, GROUP, depth))
            wide = (wide * mask).reshape(rows * GROUP, depth)
            right = jnp.concatenate(
                [jnp.concatenate(plain, axis=0), jnp.concatenate(turned, axis=0)], axis=1
            )
            result = dot_nn(wide, right).astype(jnp.bfloat16).reshape(rows, GROUP, 2 * block)
            at = pl.multiple_of(step * FCHUNK + g * GROUP, GROUP)
            cross[:, 0, pl.ds(at, GROUP), :] = result[:, :, :block]
            cross[:, 1, pl.ds(at, GROUP), :] = result[:, :, block:]

    @pl.when(step >= CROSS_STEPS)
    def _():
        base = (step - CROSS_STEPS) * ROWS_STEP
        table = table_ref[...]
        for pair in range(ROWS_STEP // 2):
            both = [
                cross[base + 2 * pair + h].reshape(2 * FREQS, block) for h in range(2)
            ]
            lagged = dot_nn(table, jnp.concatenate(both, axis=1)) * norm_factor
            for h in range(2):
                out_ref[2 * pair + h, 0] = lagged[:, h * block:(h + 1) * block].T


def stack(index, gathered, norm_factor, rows):
    _, parts, segs, _, _, block = gathered.shape
    grid = (TILE_DEV, CROSS_STEPS + rows // ROWS_STEP)
    shape = (1, parts, segs, 2, FCHUNK, block)

    def place(offset, slot, step, index_ref):
        return (index_ref[offset + slot], 0, 0, 0, jnp.minimum(step, CROSS_STEPS - 1), 0)

    return pl.pallas_call(
        functools.partial(stack_kernel, norm_factor, parts, segs, rows),
        grid_spec=pltpu.PrefetchScalarGridSpec(
            num_scalar_prefetch=1,
            grid=grid,
            in_specs=[
                pl.BlockSpec(shape, functools.partial(place, 0)),
                pl.BlockSpec(shape, functools.partial(place, TILE_DEV)),
                pl.BlockSpec((LAGS, 2 * FREQS), lambda slot, step, index_ref: (0, 0)),
            ],
            out_specs=pl.BlockSpec(
                (ROWS_STEP, 1, block, LAGS),
                lambda slot, step, index_ref: (jnp.maximum(step - CROSS_STEPS, 0), slot, 0, 0),
            ),
            scratch_shapes=[pltpu.VMEM((rows, 2, FREQS, block), jnp.bfloat16)],
        ),
        out_shape=jax.ShapeDtypeStruct((rows, TILE_DEV, block, LAGS), jnp.float32),
        compiler_params=pltpu.CompilerParams(vmem_limit_bytes=48 << 20),
    )(index, gathered, gathered, jnp.asarray(lag_table()))


def on_device(traces, pair_offsets, pair_counts, pair_owner):
    block_size, local_segs, sample_count = traces.shape
    parts_count = lax.axis_size("seg")
    block_count = lax.axis_size("chan")
    norm_factor = 1.0 / math.sqrt(FREQS * local_segs * parts_count)
    whitened, index = whiten(traces, pair_offsets, pair_counts, pair_owner)
    if (block_count, parts_count) == (8, PLANES):
        gathered = gather(whitened)
    else:
        gathered = lax.all_gather(lax.all_gather(whitened, "seg", axis=0), "chan", axis=0)
    return stack(index, gathered, norm_factor, block_size // parts_count)


def solution(mesh):
    placed = (P("chan", "seg", None), P(), P(), P())
    return jax.shard_map(
        on_device,
        mesh=mesh,
        in_specs=placed,
        out_specs=P("seg", "chan", None, None),
        check_vma=False,
    )
```

```python
import functools
import math

import jax
import jax.numpy as jnp
import ml_dtypes
import numpy as np
from jax import lax
from jax.experimental import pallas as pl
from jax.experimental.pallas import tpu as pltpu
from jax.sharding import PartitionSpec as P

SAMPLES = 8192
BAND_START = 32
FREQS = 512
HALF = 8
LAGS = 256
TILE_DEV = 2

RADIX = 8
FOLDED = SAMPLES // RADIX
RESIDUES = (0, 4, 1, 7, 2, 6, 3, 5)
PER_RES = FREQS // RADIX
LANES = 128
PARTS = FOLDED // LANES
BF16 = ml_dtypes.bfloat16

BIN_ORDER = np.concatenate([np.arange(PER_RES) * RADIX + r for r in RESIDUES])


def dft_tables():
    n = np.arange(FOLDED)
    full = np.zeros((4, 4 * PER_RES, 2, FOLDED))
    for group in range(4):
        first, second = RESIDUES[2 * group], RESIDUES[2 * group + 1]
        parts = []
        for r in (first, second):
            k = BAND_START + np.arange(PER_RES) * RADIX + r
            angle = 2.0 * np.pi / SAMPLES * ((k[:, None] * n[None, :]) % SAMPLES)
            parts.append((np.cos(angle), np.sin(angle)))
        (c0, s0), (c1, s1) = parts
        o = np.zeros_like(c0)
        if group == 0:
            rows = [(c0, o), (-s0, o), (o, c1), (o, -s1)]
        else:
            rows = [(c0, s0), (-s0, c0), (c1, -s1), (-s1, -c1)]
        for i, (a, b) in enumerate(rows):
            full[group, i * PER_RES:(i + 1) * PER_RES, 0] = a
            full[group, i * PER_RES:(i + 1) * PER_RES, 1] = b
    full = full.reshape(4, 4 * PER_RES, 2 * FOLDED).astype(np.float32)
    high = full.astype(BF16)
    low = (full - high.astype(np.float32)).astype(BF16)
    return high, low


def lag_table():
    shifts = np.arange(LAGS) - LAGS // 2
    angle = 2.0 * np.pi / SAMPLES * (((BAND_START + BIN_ORDER)[None, :] * shifts[:, None]) % SAMPLES)
    return np.concatenate([np.cos(angle), -np.sin(angle)], axis=1).astype(np.float32).astype(BF16)


def window_table():
    return (np.abs(BIN_ORDER[:, None] - BIN_ORDER[None, :]) <= HALF).astype(BF16)


def split(value):
    high = value.astype(jnp.bfloat16)
    return high, (value - high.astype(jnp.float32)).astype(jnp.bfloat16)


def dot_nt(a, b):
    return lax.dot_general(a, b, (((1,), (1,)), ((), ())), preferred_element_type=jnp.float32)


def dot_nn(a, b):
    return jnp.dot(a, b, preferred_element_type=jnp.float32)


def list_pairs(offsets_ref, counts_ref, owner_ref, index_ref):
    blocks = counts_ref.shape[0]
    my_start = lax.axis_index("chan") * TILE_DEV
    for i in range(2 * TILE_DEV):
        index_ref[i] = 0
    index_ref[2 * TILE_DEV] = lax.axis_index("seg")

    def one_block(a, start):
        def one_pair(rank, carry):
            slot = owner_ref[start + rank] - my_start

            @pl.when((slot >= 0) & (slot < TILE_DEV))
            def _():
                index_ref[slot] = a
                index_ref[TILE_DEV + slot] = lax.rem(a + offsets_ref[a, rank], blocks)

            return carry

        lax.fori_loop(0, counts_ref[a], one_pair, 0)
        return start + counts_ref[a]

    lax.fori_loop(0, blocks, one_block, 0)


def whiten_kernel(x_ref, high_ref, low_ref, near_ref, offsets_ref, counts_ref, owner_ref,
                  out_ref, index_ref, folded, total):
    step = pl.program_id(0)
    block_size = x_ref.shape[0]
    segs = out_ref.shape[0]
    deep = PARTS * segs
    some = 2

    @pl.when(step == 0)
    def _():
        list_pairs(offsets_ref, counts_ref, owner_ref, index_ref)

        def fold(i, carry):
            at = i * some
            x = [
                x_ref[pl.ds(at, some), j * deep:(j + 1) * deep, :].astype(jnp.float32)
                for j in range(RADIX)
            ]
            e0, e1, e2, e3 = x[0] + x[4], x[1] + x[5], x[2] + x[6], x[3] + x[7]
            d0, d1, d2, d3 = x[0] - x[4], x[1] - x[5], x[2] - x[6], x[3] - x[7]
            root = math.sqrt(0.5)
            plus, minus = (d1 + d3) * root, (d1 - d3) * root
            values = (
                (e0 + e2) + (e1 + e3), (e0 + e2) - (e1 + e3),
                d0 + minus, -(d2 + plus),
                e0 - e2, e3 - e1,
                d0 - minus, d2 - plus,
            )
            for j, value in enumerate(values):
                rows = pl.ds(pl.multiple_of(at * deep, some * deep), some * deep)
                folded[j // 2, j % 2, rows, :] = value.reshape(some * deep, LANES)
            return carry

        lax.fori_loop(0, block_size // some, fold, 0, unroll=2)

    pieces = []
    for half in range(2):
        for part in range(PARTS):
            column = [
                folded[step, half, pl.ds(part * segs + s, block_size, stride=deep), :]
                for s in range(segs)
            ]
            pieces.append(split(jnp.concatenate(column, axis=0)))
    y_high = jnp.concatenate([piece[0] for piece in pieces], axis=1)
    y_low = jnp.concatenate([piece[1] for piece in pieces], axis=1)
    t_high = high_ref[0]
    total[step] = dot_nt(t_high, y_high) + dot_nt(t_high, y_low) + dot_nt(low_ref[0], y_high)

    @pl.when(step == pl.num_programs(0) - 1)
    def _():
        real, imag, counts = [], [], []
        width = segs * block_size
        for group in range(4):
            for half in range(2):
                base = half * 2 * PER_RES
                real.append(total[group, base:base + PER_RES])
                imag.append(total[group, base + PER_RES:base + 2 * PER_RES])
                bins = lax.broadcasted_iota(jnp.int32, (PER_RES, width), 0) * RADIX
                bins = bins + RESIDUES[2 * group + half]
                ends = jnp.minimum(bins + HALF, FREQS - 1) - jnp.maximum(bins - HALF, 0)
                counts.append((ends + 1).astype(jnp.float32))
        real = jnp.concatenate(real, axis=0)
        imag = jnp.concatenate(imag, axis=0)
        amplitude = jnp.sqrt(real * real + imag * imag)
        high = amplitude.astype(jnp.bfloat16)
        mid, low = split(amplitude - high.astype(jnp.float32))
        near = near_ref[...]
        summed = dot_nn(near, high) + (dot_nn(near, mid) + dot_nn(near, low))
        divisor = jnp.maximum(summed / jnp.concatenate(counts, axis=0), 1.0)
        for part, value in enumerate((real, imag)):
            white = (value / divisor).astype(jnp.bfloat16)
            for s in range(segs):
                out_ref[s, part] = white[:, s * block_size:(s + 1) * block_size]


def whiten(traces, pair_offsets, pair_counts, pair_owner):
    block_size, segs, samples = traces.shape
    pieces = samples // LANES
    laid = traces.reshape(block_size, segs, pieces, LANES).transpose(0, 2, 1, 3)
    laid = laid.reshape(block_size, pieces * segs, LANES)
    high, low = dft_tables()
    once = lambda shape: pl.BlockSpec(shape, lambda g: (0,) * len(shape))
    table = pl.BlockSpec((1, 4 * PER_RES, 2 * FOLDED), lambda g: (g, 0, 0))
    scalars = pl.BlockSpec(memory_space=pltpu.SMEM)
    return pl.pallas_call(
        whiten_kernel,
        grid=(4,),
        in_specs=[once(laid.shape), table, table, once((FREQS, FREQS)), scalars, scalars, scalars],
        out_specs=[once((segs, 2, FREQS, block_size)), scalars],
        out_shape=[
            jax.ShapeDtypeStruct((segs, 2, FREQS, block_size), jnp.bfloat16),
            jax.ShapeDtypeStruct((8,), jnp.int32),
        ],
        scratch_shapes=[
            pltpu.VMEM((4, 2, block_size * PARTS * segs, LANES), jnp.float32),
            pltpu.VMEM((4, 4 * PER_RES, block_size * segs), jnp.float32),
        ],
        compiler_params=pltpu.CompilerParams(vmem_limit_bytes=56 << 20),
    )(laid, jnp.asarray(high), jnp.asarray(low), jnp.asarray(window_table()),
      pair_offsets, pair_counts, pair_owner)


PLANES = 4
MESH = pl.DeviceIdType.MESH
LINE_ROWS = 1664


def gather_kernel(own_ref, all_ref, z_send, z_recv, p_send, p_recv, c_send, c_recv,
                  bz_send, bz_recv, bp_send, bp_recv, bc_send, bc_recv, own_sem):
    chan, seg = lax.axis_index("chan"), lax.axis_index("seg")
    y, x, core = chan // 4, (chan // 2) % 2, chan % 2
    x_near = 4 * y + 2 * (1 - x) + core
    y_near = 4 * (1 - y) + 2 * x + core
    across = 4 * (1 - y) + 2 * (1 - x) + core
    twin = 4 * y + 2 * x + (1 - core)
    blocks = (chan, x_near, y_near, across)
    twin_blocks = [block + 1 - 2 * core for block in blocks]
    near = (x_near, y_near)
    total_rows = own_ref.shape[0]
    line = pl.ds(0, LINE_ROWS)
    line_half = [pl.ds(h * (LINE_ROWS // 2), LINE_ROWS // 2) for h in (0, 1)]
    rest_rows = total_rows - LINE_ROWS
    rest = pl.ds(LINE_ROWS, rest_rows)
    rest_half = [pl.ds(LINE_ROWS + h * (rest_rows // 2), rest_rows // 2) for h in (0, 1)]

    barrier = pltpu.get_barrier_semaphore()
    for other in (x_near, y_near, twin):
        pl.semaphore_signal(barrier, inc=1, device_id=(other, seg), device_id_type=MESH)

    def program(z):
        for step in (1, -1):
            if 0 <= z + step < PLANES:
                pl.semaphore_signal(barrier, inc=1, device_id=(chan, z + step), device_id_type=MESH)
        pl.semaphore_wait(barrier, 3 + int(z > 0) + int(z < PLANES - 1))
        sent = []
        order = sorted(range(PLANES), key=lambda other: abs(other - z))

        def send(src, dst, send_sem, recv_sem, device):
            copy = pltpu.make_async_remote_copy(
                src_ref=src, dst_ref=dst, send_sem=send_sem, recv_sem=recv_sem,
                device_id=device, device_id_type=MESH,
            )
            copy.start()
            sent.append(copy)

        def landed(ref, sem):
            pltpu.make_async_remote_copy(
                src_ref=ref, dst_ref=ref, send_sem=sem, recv_sem=sem,
                device_id=(twin, z), device_id_type=MESH,
            ).wait_recv()

        def part(block, other, rows):
            if block == 0 and other == z:
                return own_ref.at[rows]
            return all_ref.at[blocks[block], other, rows]

        def along(block, other, rows, send_sem, recv_sem):
            for step, side in ((1, 0), (-1, 1)):
                away = other == z or (z - other) * step > 0
                if away and 0 <= z + step < PLANES:
                    send(part(block, other, rows), all_ref.at[blocks[block], other, rows],
                         send_sem.at[other, block, side], recv_sem.at[other, block], (chan, z + step))

        def to_twin(block, other, rows, send_sem, recv_sem, half):
            send(part(block, other, rows), all_ref.at[blocks[block], other, rows],
                 send_sem.at[other, block, half], recv_sem.at[other, block, half], (twin, z))

        def outward(other, halves, send_sem, recv_sem):
            for first in (0, 1):
                for way in (0, 1):
                    half = first if way == 0 else 1 - first
                    send(part(0, other, halves[half]), all_ref.at[chan, other, halves[half]],
                         send_sem.at[other, way, half], recv_sem.at[other, way, half], (near[way], z))

        def onward(other, halves, send_sem, recv_sem, first):
            for way in (0, 1):
                half = first if way == 0 else 1 - first
                ref = all_ref.at[near[way], other, halves[half]]
                landed(ref, recv_sem.at[other, way, half])
                if half == way:
                    send(ref, ref, send_sem.at[other, 2, half], recv_sem.at[other, 2, half],
                         (near[1 - way], z))

        def finish(other, halves, recv_sem):
            for half in (0, 1):
                landed(all_ref.at[across, other, halves[half]], recv_sem.at[other, 2, half])

        def line_out(other):
            outward(other, line_half, p_send, p_recv)
            for half in (0, 1):
                to_twin(0, other, line_half[half], c_send, c_recv, half)

        def line_on(other):
            for first in (0, 1):
                onward(other, line_half, p_send, p_recv, first)
                to_twin(1, other, line_half[first], c_send, c_recv, first)
                to_twin(2, other, line_half[1 - first], c_send, c_recv, 1 - first)

        def line_finish(other):
            finish(other, line_half, p_recv)
            for half in (0, 1):
                to_twin(3, other, line_half[half], c_send, c_recv, half)

        def rest_line(other):
            for block in range(4):
                landed(all_ref.at[blocks[block], other, rest], bz_recv.at[other, block])
                along(block, other, rest, bz_send, bz_recv)
                to_twin(block, other, rest, bc_send, bc_recv, 0)

        along(0, z, line, z_send, z_recv)
        outward(z, rest_half, bp_send, bp_recv)
        to_twin(0, z, rest, bc_send, bc_recv, 0)
        local = pltpu.make_async_copy(own_ref, all_ref.at[chan, z], own_sem)
        local.start()
        line_out(z)
        for first in (0, 1):
            onward(z, rest_half, bp_send, bp_recv, first)
        for block in (1, 2):
            to_twin(block, z, rest, bc_send, bc_recv, 0)
        for k in range(1, PLANES):
            landed(all_ref.at[chan, order[k], line], z_recv.at[order[k], 0])
            along(0, order[k], line, z_send, z_recv)
            line_out(order[k])
            if k == 1:
                finish(z, rest_half, bp_recv)
                to_twin(3, z, rest, bc_send, bc_recv, 0)
            if k == PLANES - 1:
                for block in range(4):
                    along(block, z, rest, bz_send, bz_recv)
            line_on(order[k - 1])
            if k > 1:
                line_finish(order[k - 2])
        rest_line(order[1])
        rest_line(order[2])
        line_on(order[-1])
        line_finish(order[-2])
        line_finish(order[-1])
        rest_line(order[3])
        for other in range(PLANES):
            for block in range(4):
                ref = all_ref.at[twin_blocks[block], other]
                for half in (0, 1):
                    landed(ref.at[line_half[half]], c_recv.at[other, block, half])
                landed(ref.at[rest], bc_recv.at[other, block, 0])
        for copy in sent:
            copy.wait_send()
        local.wait()

    for z in range(PLANES):
        pl.when(seg == z)(functools.partial(program, z))


def gather(own):
    dma = pltpu.SemaphoreType.DMA
    rows, lanes = math.prod(own.shape[:-1]), own.shape[-1]
    gathered = pl.pallas_call(
        gather_kernel,
        in_specs=[pl.BlockSpec(memory_space=pl.ANY)],
        out_specs=pl.BlockSpec(memory_space=pl.ANY),
        out_shape=jax.ShapeDtypeStruct((8, PLANES, rows, lanes), own.dtype),
        scratch_shapes=[
            dma((PLANES, 1, 2)), dma((PLANES, 1)),
            dma((PLANES, 3, 2)), dma((PLANES, 3, 2)),
            dma((PLANES, 4, 2)), dma((PLANES, 4, 2)),
            dma((PLANES, 4, 2)), dma((PLANES, 4)),
            dma((PLANES, 3, 2)), dma((PLANES, 3, 2)),
            dma((PLANES, 4, 1)), dma((PLANES, 4, 1)), dma,
        ],
        compiler_params=pltpu.CompilerParams(collective_id=0, has_side_effects=True),
    )(own.reshape(rows, lanes))
    return gathered.reshape((8, PLANES) + own.shape)


GROUP = 16
FCHUNK = 256
CROSS_STEPS = FREQS // FCHUNK
ROWS_STEP = 16


def stack_kernel(norm_factor, parts, segs, rows, index_ref, first_ref, second_ref, table_ref, out_ref, cross):
    step = pl.program_id(1)
    depth = parts * segs * 2 * GROUP
    block = second_ref.shape[-1]

    @pl.when(step < CROSS_STEPS)
    def _():
        own = index_ref[4] * rows
        select = (
            lax.broadcasted_iota(jnp.int32, (rows, block), 1)
            == lax.broadcasted_iota(jnp.int32, (rows, block), 0) + own
        ).astype(jnp.bfloat16)
        mask = (
            lax.broadcasted_iota(jnp.int32, (rows, GROUP, depth), 2) % GROUP
            == lax.broadcasted_iota(jnp.int32, (rows, GROUP, depth), 1)
        )
        for g in range(FCHUNK // GROUP):
            span = slice(g * GROUP, (g + 1) * GROUP)
            firsts, plain, turned = [], [], []
            for z in range(parts):
                for s in range(segs):
                    firsts += [first_ref[0, z, s, p, span] for p in range(2)]
                    re, im = second_ref[0, z, s, 0, span], second_ref[0, z, s, 1, span]
                    plain += [re, im]
                    turned += [-im, re]
            left = dot_nt(select, jnp.concatenate(firsts, axis=0))
            wide = jnp.broadcast_to(left[:, None, :], (rows, GROUP, depth))
            wide = jnp.where(mask, wide, 0.0).reshape(rows * GROUP, depth).astype(jnp.bfloat16)
            right = jnp.concatenate(
                [jnp.concatenate(plain, axis=0), jnp.concatenate(turned, axis=0)], axis=1
            )
            result = dot_nn(wide, right).astype(jnp.bfloat16).reshape(rows, GROUP, 2 * block)
            at = pl.multiple_of(step * FCHUNK + g * GROUP, GROUP)
            cross[:, 0, pl.ds(at, GROUP), :] = result[:, :, :block]
            cross[:, 1, pl.ds(at, GROUP), :] = result[:, :, block:]

    @pl.when(step >= CROSS_STEPS)
    def _():
        base = (step - CROSS_STEPS) * ROWS_STEP
        table = table_ref[...]
        for pair in range(ROWS_STEP // 2):
            both = [
                cross[base + 2 * pair + h].reshape(2 * FREQS, block) for h in range(2)
            ]
            lagged = dot_nn(table, jnp.concatenate(both, axis=1)) * norm_factor
            for h in range(2):
                out_ref[2 * pair + h, 0] = lagged[:, h * block:(h + 1) * block].T


def stack(index, gathered, norm_factor, rows):
    _, parts, segs, _, _, block = gathered.shape
    grid = (TILE_DEV, CROSS_STEPS + rows // ROWS_STEP)
    shape = (1, parts, segs, 2, FCHUNK, block)

    def place(offset, slot, step, index_ref):
        return (index_ref[offset + slot], 0, 0, 0, jnp.minimum(step, CROSS_STEPS - 1), 0)

    return pl.pallas_call(
        functools.partial(stack_kernel, norm_factor, parts, segs, rows),
        grid_spec=pltpu.PrefetchScalarGridSpec(
            num_scalar_prefetch=1,
            grid=grid,
            in_specs=[
                pl.BlockSpec(shape, functools.partial(place, 0)),
                pl.BlockSpec(shape, functools.partial(place, TILE_DEV)),
                pl.BlockSpec((LAGS, 2 * FREQS), lambda slot, step, index_ref: (0, 0)),
            ],
            out_specs=pl.BlockSpec(
                (ROWS_STEP, 1, block, LAGS),
                lambda slot, step, index_ref: (jnp.maximum(step - CROSS_STEPS, 0), slot, 0, 0),
            ),
            scratch_shapes=[pltpu.VMEM((rows, 2, FREQS, block), jnp.bfloat16)],
        ),
        out_shape=jax.ShapeDtypeStruct((rows, TILE_DEV, block, LAGS), jnp.float32),
        compiler_params=pltpu.CompilerParams(vmem_limit_bytes=48 << 20),
    )(index, gathered, gathered, jnp.asarray(lag_table()))


def on_device(traces, pair_offsets, pair_counts, pair_owner):
    block_size, local_segs, sample_count = traces.shape
    parts_count = lax.axis_size("seg")
    block_count = lax.axis_size("chan")
    norm_factor = 1.0 / math.sqrt(FREQS * local_segs * parts_count)
    whitened, index = whiten(traces, pair_offsets, pair_counts, pair_owner)
    if (block_count, parts_count) == (8, PLANES):
        gathered = gather(whitened)
    else:
        gathered = lax.all_gather(lax.all_gather(whitened, "seg", axis=0), "chan", axis=0)
    return stack(index, gathered, norm_factor, block_size // parts_count)


def solution(mesh):
    placed = (P("chan", "seg", None), P(), P(), P())
    return jax.shard_map(
        on_device,
        mesh=mesh,
        in_specs=placed,
        out_specs=P("seg", "chan", None, None),
        check_vma=False,
    )
```

```python
import functools
import math

import jax
import jax.numpy as jnp
import ml_dtypes
import numpy as np
from jax import lax
from jax.experimental import pallas as pl
from jax.experimental.pallas import tpu as pltpu
from jax.sharding import PartitionSpec as P

SAMPLES = 8192
BAND_START = 32
FREQS = 512
HALF = 8
LAGS = 256
TILE_DEV = 2

RADIX = 8
FOLDED = SAMPLES // RADIX
RESIDUES = (0, 4, 1, 7, 2, 6, 3, 5)
PER_RES = FREQS // RADIX
LANES = 128
PARTS = FOLDED // LANES
BF16 = ml_dtypes.bfloat16

BIN_ORDER = np.concatenate([np.arange(PER_RES) * RADIX + r for r in RESIDUES])


def dft_tables():
    n = np.arange(FOLDED)
    full = np.zeros((4, 4 * PER_RES, 2, FOLDED))
    for group in range(4):
        first, second = RESIDUES[2 * group], RESIDUES[2 * group + 1]
        parts = []
        for r in (first, second):
            k = BAND_START + np.arange(PER_RES) * RADIX + r
            angle = 2.0 * np.pi / SAMPLES * ((k[:, None] * n[None, :]) % SAMPLES)
            parts.append((np.cos(angle), np.sin(angle)))
        (c0, s0), (c1, s1) = parts
        o = np.zeros_like(c0)
        if group == 0:
            rows = [(c0, o), (-s0, o), (o, c1), (o, -s1)]
        else:
            rows = [(c0, s0), (-s0, c0), (c1, -s1), (-s1, -c1)]
        for i, (a, b) in enumerate(rows):
            full[group, i * PER_RES:(i + 1) * PER_RES, 0] = a
            full[group, i * PER_RES:(i + 1) * PER_RES, 1] = b
    full = full.reshape(4, 4 * PER_RES, 2 * FOLDED).astype(np.float32)
    high = full.astype(BF16)
    low = (full - high.astype(np.float32)).astype(BF16)
    return high, low


def lag_table():
    shifts = np.arange(LAGS) - LAGS // 2
    angle = 2.0 * np.pi / SAMPLES * (((BAND_START + BIN_ORDER)[None, :] * shifts[:, None]) % SAMPLES)
    return np.concatenate([np.cos(angle), -np.sin(angle)], axis=1).astype(np.float32).astype(BF16)


def window_table():
    return (np.abs(BIN_ORDER[:, None] - BIN_ORDER[None, :]) <= HALF).astype(BF16)


def split(value):
    high = value.astype(jnp.bfloat16)
    return high, (value - high.astype(jnp.float32)).astype(jnp.bfloat16)


def dot_nt(a, b):
    return lax.dot_general(a, b, (((1,), (1,)), ((), ())), preferred_element_type=jnp.float32)


def dot_nn(a, b):
    return jnp.dot(a, b, preferred_element_type=jnp.float32)


def list_pairs(offsets_ref, counts_ref, owner_ref, index_ref):
    blocks = counts_ref.shape[0]
    my_start = lax.axis_index("chan") * TILE_DEV
    for i in range(2 * TILE_DEV):
        index_ref[i] = 0
    index_ref[2 * TILE_DEV] = lax.axis_index("seg")

    def one_block(a, start):
        def one_pair(rank, carry):
            slot = owner_ref[start + rank] - my_start

            @pl.when((slot >= 0) & (slot < TILE_DEV))
            def _():
                index_ref[slot] = a
                index_ref[TILE_DEV + slot] = lax.rem(a + offsets_ref[a, rank], blocks)

            return carry

        lax.fori_loop(0, counts_ref[a], one_pair, 0)
        return start + counts_ref[a]

    lax.fori_loop(0, blocks, one_block, 0)


def whiten_kernel(x_ref, high_ref, low_ref, near_ref, offsets_ref, counts_ref, owner_ref,
                  out_ref, index_ref, folded, total):
    step = pl.program_id(0)
    block_size = x_ref.shape[0]
    segs = out_ref.shape[0]
    deep = PARTS * segs
    some = 2

    @pl.when(step == 0)
    def _():
        list_pairs(offsets_ref, counts_ref, owner_ref, index_ref)

        def fold(i, carry):
            at = i * some
            x = [
                x_ref[pl.ds(at, some), j * deep:(j + 1) * deep, :].astype(jnp.float32)
                for j in range(RADIX)
            ]
            e0, e1, e2, e3 = x[0] + x[4], x[1] + x[5], x[2] + x[6], x[3] + x[7]
            d0, d1, d2, d3 = x[0] - x[4], x[1] - x[5], x[2] - x[6], x[3] - x[7]
            root = math.sqrt(0.5)
            plus, minus = (d1 + d3) * root, (d1 - d3) * root
            values = (
                (e0 + e2) + (e1 + e3), (e0 + e2) - (e1 + e3),
                d0 + minus, -(d2 + plus),
                e0 - e2, e3 - e1,
                d0 - minus, d2 - plus,
            )
            for j, value in enumerate(values):
                rows = pl.ds(pl.multiple_of(at * deep, some * deep), some * deep)
                folded[j // 2, j % 2, rows, :] = value.reshape(some * deep, LANES)
            return carry

        lax.fori_loop(0, block_size // some, fold, 0, unroll=2)

    pieces = []
    for half in range(2):
        for part in range(PARTS):
            column = [
                folded[step, half, pl.ds(part * segs + s, block_size, stride=deep), :]
                for s in range(segs)
            ]
            pieces.append(split(jnp.concatenate(column, axis=0)))
    y_high = jnp.concatenate([piece[0] for piece in pieces], axis=1)
    y_low = jnp.concatenate([piece[1] for piece in pieces], axis=1)
    t_high = high_ref[0]
    total[step] = dot_nt(t_high, y_high) + dot_nt(t_high, y_low) + dot_nt(low_ref[0], y_high)

    @pl.when(step == pl.num_programs(0) - 1)
    def _():
        real, imag, counts = [], [], []
        width = segs * block_size
        for group in range(4):
            for half in range(2):
                base = half * 2 * PER_RES
                real.append(total[group, base:base + PER_RES])
                imag.append(total[group, base + PER_RES:base + 2 * PER_RES])
                bins = lax.broadcasted_iota(jnp.int32, (PER_RES, width), 0) * RADIX
                bins = bins + RESIDUES[2 * group + half]
                ends = jnp.minimum(bins + HALF, FREQS - 1) - jnp.maximum(bins - HALF, 0)
                counts.append((ends + 1).astype(jnp.float32))
        real = jnp.concatenate(real, axis=0)
        imag = jnp.concatenate(imag, axis=0)
        amplitude = jnp.sqrt(real * real + imag * imag)
        high = amplitude.astype(jnp.bfloat16)
        mid, low = split(amplitude - high.astype(jnp.float32))
        near = near_ref[...]
        summed = dot_nn(near, high) + (dot_nn(near, mid) + dot_nn(near, low))
        divisor = jnp.maximum(summed / jnp.concatenate(counts, axis=0), 1.0)
        for part, value in enumerate((real, imag)):
            white = (value / divisor).astype(jnp.bfloat16)
            for s in range(segs):
                out_ref[s, part] = white[:, s * block_size:(s + 1) * block_size]


def whiten(traces, pair_offsets, pair_counts, pair_owner):
    block_size, segs, samples = traces.shape
    pieces = samples // LANES
    laid = traces.reshape(block_size, segs, pieces, LANES).transpose(0, 2, 1, 3)
    laid = laid.reshape(block_size, pieces * segs, LANES)
    high, low = dft_tables()
    once = lambda shape: pl.BlockSpec(shape, lambda g: (0,) * len(shape))
    table = pl.BlockSpec((1, 4 * PER_RES, 2 * FOLDED), lambda g: (g, 0, 0))
    scalars = pl.BlockSpec(memory_space=pltpu.SMEM)
    return pl.pallas_call(
        whiten_kernel,
        grid=(4,),
        in_specs=[once(laid.shape), table, table, once((FREQS, FREQS)), scalars, scalars, scalars],
        out_specs=[once((segs, 2, FREQS, block_size)), scalars],
        out_shape=[
            jax.ShapeDtypeStruct((segs, 2, FREQS, block_size), jnp.bfloat16),
            jax.ShapeDtypeStruct((8,), jnp.int32),
        ],
        scratch_shapes=[
            pltpu.VMEM((4, 2, block_size * PARTS * segs, LANES), jnp.float32),
            pltpu.VMEM((4, 4 * PER_RES, block_size * segs), jnp.float32),
        ],
        compiler_params=pltpu.CompilerParams(vmem_limit_bytes=56 << 20),
    )(laid, jnp.asarray(high), jnp.asarray(low), jnp.asarray(window_table()),
      pair_offsets, pair_counts, pair_owner)


PLANES = 4
MESH = pl.DeviceIdType.MESH
LINE_ROWS = 1792


def gather_kernel(own_ref, all_ref, z_send, z_recv, p_send, p_recv, c_send, c_recv,
                  bz_send, bz_recv, bp_send, bp_recv, bc_send, bc_recv, own_sem):
    chan, seg = lax.axis_index("chan"), lax.axis_index("seg")
    y, x, core = chan // 4, (chan // 2) % 2, chan % 2
    x_near = 4 * y + 2 * (1 - x) + core
    y_near = 4 * (1 - y) + 2 * x + core
    across = 4 * (1 - y) + 2 * (1 - x) + core
    twin = 4 * y + 2 * x + (1 - core)
    blocks = (chan, x_near, y_near, across)
    twin_blocks = [block + 1 - 2 * core for block in blocks]
    near = (x_near, y_near)
    total_rows = own_ref.shape[0]
    line = pl.ds(0, LINE_ROWS)
    line_half = [pl.ds(h * (LINE_ROWS // 2), LINE_ROWS // 2) for h in (0, 1)]
    rest_rows = total_rows - LINE_ROWS
    rest = pl.ds(LINE_ROWS, rest_rows)
    rest_half = [pl.ds(LINE_ROWS + h * (rest_rows // 2), rest_rows // 2) for h in (0, 1)]

    barrier = pltpu.get_barrier_semaphore()
    for other in (x_near, y_near, twin):
        pl.semaphore_signal(barrier, inc=1, device_id=(other, seg), device_id_type=MESH)

    def program(z):
        for step in (1, -1):
            if 0 <= z + step < PLANES:
                pl.semaphore_signal(barrier, inc=1, device_id=(chan, z + step), device_id_type=MESH)
        pl.semaphore_wait(barrier, 3 + int(z > 0) + int(z < PLANES - 1))
        sent = []
        order = sorted(range(PLANES), key=lambda other: abs(other - z))

        def send(src, dst, send_sem, recv_sem, device):
            copy = pltpu.make_async_remote_copy(
                src_ref=src, dst_ref=dst, send_sem=send_sem, recv_sem=recv_sem,
                device_id=device, device_id_type=MESH,
            )
            copy.start()
            sent.append(copy)

        def landed(ref, sem):
            pltpu.make_async_remote_copy(
                src_ref=ref, dst_ref=ref, send_sem=sem, recv_sem=sem,
                device_id=(twin, z), device_id_type=MESH,
            ).wait_recv()

        def part(block, other, rows):
            if block == 0 and other == z:
                return own_ref.at[rows]
            return all_ref.at[blocks[block], other, rows]

        def along(block, other, rows, send_sem, recv_sem):
            for step, side in ((1, 0), (-1, 1)):
                away = other == z or (z - other) * step > 0
                if away and 0 <= z + step < PLANES:
                    send(part(block, other, rows), all_ref.at[blocks[block], other, rows],
                         send_sem.at[other, block, side], recv_sem.at[other, block], (chan, z + step))

        def to_twin(block, other, rows, send_sem, recv_sem, half):
            send(part(block, other, rows), all_ref.at[blocks[block], other, rows],
                 send_sem.at[other, block, half], recv_sem.at[other, block, half], (twin, z))

        def outward(other, halves, send_sem, recv_sem):
            for first in (0, 1):
                for way in (0, 1):
                    half = first if way == 0 else 1 - first
                    send(part(0, other, halves[half]), all_ref.at[chan, other, halves[half]],
                         send_sem.at[other, way, half], recv_sem.at[other, way, half], (near[way], z))

        def onward(other, halves, send_sem, recv_sem, first):
            for way in (0, 1):
                half = first if way == 0 else 1 - first
                ref = all_ref.at[near[way], other, halves[half]]
                landed(ref, recv_sem.at[other, way, half])
                if half == way:
                    send(ref, ref, send_sem.at[other, 2, half], recv_sem.at[other, 2, half],
                         (near[1 - way], z))

        def finish(other, halves, recv_sem):
            for half in (0, 1):
                landed(all_ref.at[across, other, halves[half]], recv_sem.at[other, 2, half])

        def line_out(other):
            outward(other, line_half, p_send, p_recv)
            for half in (0, 1):
                to_twin(0, other, line_half[half], c_send, c_recv, half)

        def line_on(other):
            for first in (0, 1):
                onward(other, line_half, p_send, p_recv, first)
                to_twin(1, other, line_half[first], c_send, c_recv, first)
                to_twin(2, other, line_half[1 - first], c_send, c_recv, 1 - first)

        def line_finish(other):
            finish(other, line_half, p_recv)
            for half in (0, 1):
                to_twin(3, other, line_half[half], c_send, c_recv, half)

        def rest_line(other):
            for block in range(4):
                landed(all_ref.at[blocks[block], other, rest], bz_recv.at[other, block])
                along(block, other, rest, bz_send, bz_recv)
                to_twin(block, other, rest, bc_send, bc_recv, 0)

        along(0, z, line, z_send, z_recv)
        outward(z, rest_half, bp_send, bp_recv)
        along(0, z, rest, bz_send, bz_recv)
        to_twin(0, z, rest, bc_send, bc_recv, 0)
        local = pltpu.make_async_copy(own_ref, all_ref.at[chan, z], own_sem)
        local.start()
        line_out(z)
        for first in (0, 1):
            onward(z, rest_half, bp_send, bp_recv, first)
        for block in (1, 2):
            along(block, z, rest, bz_send, bz_recv)
            to_twin(block, z, rest, bc_send, bc_recv, 0)
        finish(z, rest_half, bp_recv)
        along(3, z, rest, bz_send, bz_recv)
        to_twin(3, z, rest, bc_send, bc_recv, 0)
        for k in range(1, PLANES):
            landed(all_ref.at[chan, order[k], line], z_recv.at[order[k], 0])
            along(0, order[k], line, z_send, z_recv)
            line_out(order[k])
            line_on(order[k - 1])
            rest_line(order[k])
            if k > 1:
                line_finish(order[k - 2])
        line_on(order[-1])
        line_finish(order[-2])
        line_finish(order[-1])
        for other in range(PLANES):
            for block in range(4):
                ref = all_ref.at[twin_blocks[block], other]
                for half in (0, 1):
                    landed(ref.at[line_half[half]], c_recv.at[other, block, half])
                landed(ref.at[rest], bc_recv.at[other, block, 0])
        for copy in sent:
            copy.wait_send()
        local.wait()

    for z in range(PLANES):
        pl.when(seg == z)(functools.partial(program, z))


def gather(own):
    dma = pltpu.SemaphoreType.DMA
    rows, lanes = math.prod(own.shape[:-1]), own.shape[-1]
    gathered = pl.pallas_call(
        gather_kernel,
        in_specs=[pl.BlockSpec(memory_space=pl.ANY)],
        out_specs=pl.BlockSpec(memory_space=pl.ANY),
        out_shape=jax.ShapeDtypeStruct((8, PLANES, rows, lanes), own.dtype),
        scratch_shapes=[
            dma((PLANES, 1, 2)), dma((PLANES, 1)),
            dma((PLANES, 3, 2)), dma((PLANES, 3, 2)),
            dma((PLANES, 4, 2)), dma((PLANES, 4, 2)),
            dma((PLANES, 4, 2)), dma((PLANES, 4)),
            dma((PLANES, 3, 2)), dma((PLANES, 3, 2)),
            dma((PLANES, 4, 1)), dma((PLANES, 4, 1)), dma,
        ],
        compiler_params=pltpu.CompilerParams(collective_id=0, has_side_effects=True),
    )(own.reshape(rows, lanes))
    return gathered.reshape((8, PLANES) + own.shape)


GROUP = 16
FCHUNK = 256
CROSS_STEPS = FREQS // FCHUNK
ROWS_STEP = 16


def stack_kernel(norm_factor, parts, segs, rows, index_ref, first_ref, second_ref, table_ref, out_ref, cross):
    step = pl.program_id(1)
    depth = parts * segs * 2 * GROUP
    block = second_ref.shape[-1]

    @pl.when(step < CROSS_STEPS)
    def _():
        own = index_ref[4] * rows
        select = (
            lax.broadcasted_iota(jnp.int32, (rows, block), 1)
            == lax.broadcasted_iota(jnp.int32, (rows, block), 0) + own
        ).astype(jnp.bfloat16)
        mask = (
            lax.broadcasted_iota(jnp.int32, (rows, GROUP, depth), 2) % GROUP
            == lax.broadcasted_iota(jnp.int32, (rows, GROUP, depth), 1)
        )
        for g in range(FCHUNK // GROUP):
            span = slice(g * GROUP, (g + 1) * GROUP)
            firsts, plain, turned = [], [], []
            for z in range(parts):
                for s in range(segs):
                    firsts += [first_ref[0, z, s, p, span] for p in range(2)]
                    re, im = second_ref[0, z, s, 0, span], second_ref[0, z, s, 1, span]
                    plain += [re, im]
                    turned += [-im, re]
            left = dot_nt(select, jnp.concatenate(firsts, axis=0))
            wide = jnp.broadcast_to(left[:, None, :], (rows, GROUP, depth))
            wide = jnp.where(mask, wide, 0.0).reshape(rows * GROUP, depth).astype(jnp.bfloat16)
            right = jnp.concatenate(
                [jnp.concatenate(plain, axis=0), jnp.concatenate(turned, axis=0)], axis=1
            )
            result = dot_nn(wide, right).astype(jnp.bfloat16).reshape(rows, GROUP, 2 * block)
            at = pl.multiple_of(step * FCHUNK + g * GROUP, GROUP)
            cross[:, 0, pl.ds(at, GROUP), :] = result[:, :, :block]
            cross[:, 1, pl.ds(at, GROUP), :] = result[:, :, block:]

    @pl.when(step >= CROSS_STEPS)
    def _():
        base = (step - CROSS_STEPS) * ROWS_STEP
        table = table_ref[...]
        for pair in range(ROWS_STEP // 2):
            both = [
                cross[base + 2 * pair + h].reshape(2 * FREQS, block) for h in range(2)
            ]
            lagged = dot_nn(table, jnp.concatenate(both, axis=1)) * norm_factor
            for h in range(2):
                out_ref[2 * pair + h, 0] = lagged[:, h * block:(h + 1) * block].T


def stack(index, gathered, norm_factor, rows):
    _, parts, segs, _, _, block = gathered.shape
    grid = (TILE_DEV, CROSS_STEPS + rows // ROWS_STEP)
    shape = (1, parts, segs, 2, FCHUNK, block)

    def place(offset, slot, step, index_ref):
        return (index_ref[offset + slot], 0, 0, 0, jnp.minimum(step, CROSS_STEPS - 1), 0)

    return pl.pallas_call(
        functools.partial(stack_kernel, norm_factor, parts, segs, rows),
        grid_spec=pltpu.PrefetchScalarGridSpec(
            num_scalar_prefetch=1,
            grid=grid,
            in_specs=[
                pl.BlockSpec(shape, functools.partial(place, 0)),
                pl.BlockSpec(shape, functools.partial(place, TILE_DEV)),
                pl.BlockSpec((LAGS, 2 * FREQS), lambda slot, step, index_ref: (0, 0)),
            ],
            out_specs=pl.BlockSpec(
                (ROWS_STEP, 1, block, LAGS),
                lambda slot, step, index_ref: (jnp.maximum(step - CROSS_STEPS, 0), slot, 0, 0),
            ),
            scratch_shapes=[pltpu.VMEM((rows, 2, FREQS, block), jnp.bfloat16)],
        ),
        out_shape=jax.ShapeDtypeStruct((rows, TILE_DEV, block, LAGS), jnp.float32),
        compiler_params=pltpu.CompilerParams(vmem_limit_bytes=48 << 20),
    )(index, gathered, gathered, jnp.asarray(lag_table()))


def on_device(traces, pair_offsets, pair_counts, pair_owner):
    block_size, local_segs, sample_count = traces.shape
    parts_count = lax.axis_size("seg")
    block_count = lax.axis_size("chan")
    norm_factor = 1.0 / math.sqrt(FREQS * local_segs * parts_count)
    whitened, index = whiten(traces, pair_offsets, pair_counts, pair_owner)
    if (block_count, parts_count) == (8, PLANES):
        gathered = gather(whitened)
    else:
        gathered = lax.all_gather(lax.all_gather(whitened, "seg", axis=0), "chan", axis=0)
    return stack(index, gathered, norm_factor, block_size // parts_count)


def solution(mesh):
    placed = (P("chan", "seg", None), P(), P(), P())
    return jax.shard_map(
        on_device,
        mesh=mesh,
        in_specs=placed,
        out_specs=P("seg", "chan", None, None),
        check_vma=False,
    )
```
